128 devices in a mesh: row: 16 (over x_lo, z, core), col: 8 (over x_hi, y).
Axes of the slice: x: 4 (x_hi: 2, x_lo: 2; x = x_hi * 2 + x_lo), y: 4, z: 4, core: 2. Of those that a mesh axis runs over, the one named last changes fastest.
Arguments:
- pair: bfloat16 [1024, 1024, 128], P('row', 'col'), may hold values from -6 to 6
- chain_ids: int32 [1024], replicated, may hold values from 0 to 7, never falling along the last dimension, each value on 1 to 256 neighbouring positions
- block_mask: int32 [8, 8], replicated, may hold values 0 or 1
- w_query: bfloat16 [128, 128], replicated, may hold values from -0.5 to 0.5
- w_key: bfloat16 [128, 128], replicated, may hold values from -0.5 to 0.5
- w_value: bfloat16 [128, 128], replicated, may hold values from -0.5 to 0.5
- w_gate: bfloat16 [128, 128], replicated, may hold values from -0.5 to 0.5
- w_bias: bfloat16 [128, 4], replicated, may hold values from -19.091883 to 19.091883
- w_out: bfloat16 [128, 128], replicated, may hold values from -0.5 to 0.5
Outputs:
- update_columns: bfloat16 [8, 16, 8, 1024, 128], P('col', 'row')
The draws below stay inside these ranges and needn't reach their ends.
All inputs are finite; a program needn't handle non-finite values.
Results may differ from the reference program's by a relative error of at most 0.0095.
The reference program's roundings to bfloat16 on the way count: a program that leaves them out, or rounds other values in their place, can miss the bound.
Values may be sent and summed in bfloat16 or wider, within the bound.
No kernel may reach another device: no remote copies, remote signals or barrier semaphores. Data moves between devices by JAX's collectives and lax.ppermute only.
A program may use at most 128 MiB of HBM per device.

```python
import math
import jax
import jax.numpy as jnp
import numpy as np
from jax import lax

C = 128
H = 4
HD = 32
TILE = 128
N = 1024
CPD = 8
NT = 8
N_ROW = 16
N_COL = 8


def draw_w_bias(key, part):
    key = jax.random.fold_in(key, 11)
    raw_draw = jnp.clip(jax.random.normal(key, (C, H), jnp.float32), -4.0, 4.0)
    return (raw_draw / jnp.sqrt(jnp.float32(C))).astype(jnp.bfloat16)


def touch_ends(array, own_key, low, largest):
    longest = array.shape.index(max(array.shape))
    spots = []
    for shift in (0, 1):
        where = [jax.random.randint(jax.random.fold_in(own_key, axis), (), 0, length) for axis, length in enumerate(array.shape)]
        where[longest] = (where[longest] + shift) % array.shape[longest]
        spots.append(tuple(where))
    return array.at[spots[0]].set(low).at[spots[1]].set(largest)


def shard_levels(stream_key, dims, pieces, smallest, high):
    level = 1.0
    for axis_at, parts in pieces:
        heights = jax.random.uniform(jax.random.fold_in(jax.random.fold_in(stream_key, 6), axis_at), (parts,), jnp.float32, smallest / len(pieces), high / len(pieces))
        level = level * jnp.repeat(jnp.exp(heights), dims[axis_at] // parts).reshape((-1,) + (1,) * (len(dims) - 1 - axis_at))
    return level


def length_profile(count, total, most, slope):
    weights = [(1 << 20) // math.isqrt(rank ** slope) + 1 for rank in range(2, count + 1)]
    spare, holding = total - most - (count - 1), [1] * (count - 1)
    while spare > 0:
        movable = [i for i in range(count - 1) if holding[i] < most]
        pool, budget = sum([weights[i] for i in movable]), spare
        for i in movable:
            extra = min(most - holding[i], max(1, budget * weights[i] // pool), spare)
            holding[i] = holding[i] + extra
            spare = spare - extra
    return np.array([most] + holding)


def uneven(rng, count, total, limit, slope):
    if count == 2:
        one = jax.random.randint(rng, (), max(1, total - limit), min(limit, total - 1) + 1)
        return jnp.stack([one, total - one])
    tallies = jnp.asarray(length_profile(count, total, limit, slope), jnp.int32)
    twos = (count - 1) // 2
    giver, taker = tallies[1:1 + 2 * twos:2], tallies[2:2 + 2 * twos:2]
    margin = jnp.minimum(giver - 1, limit - taker)
    moved = jax.random.randint(jax.random.fold_in(rng, 1), (twos,), 0, 1 << 20) % (margin + 1)
    tallies = tallies.at[1:1 + 2 * twos:2].set(giver - moved).at[2:2 + 2 * twos:2].set(taker + moved)
    return tallies[jax.random.permutation(jax.random.fold_in(rng, 2), count)]


def gaussian(key, shape, deviation, limit, split=(), kind=jnp.bfloat16):
    values = jax.random.normal(key, shape, jnp.float32) * deviation
    if len(split) > 0:
        values = shard_levels(key, shape, split, -0.22, 0.18) * values
    return jnp.clip(values, min=-limit, max=limit).astype(kind)


def setup_inputs(seed: int = 0) -> dict:
    splits = jax.random.split(jax.random.key(seed), 10)
    pair = gaussian(splits[0], (N, N, C), 1.0, 6.0, ((0, 16), (1, 8)))
    chain_ids = jnp.searchsorted(jnp.cumsum(uneven(splits[1], 8, N, N // 4, 1)), jnp.arange(N), side="right").astype(jnp.int32)
    block_mask = touch_ends((jax.random.randint(splits[2], (NT, NT), 0, 2) < 1).astype(jnp.int32), jax.random.fold_in(splits[2], 1), 0, 1)
    w_query = gaussian(splits[3], (C, H * HD), C ** -0.5, 0.5)
    w_key = gaussian(splits[4], (C, H * HD), C ** -0.5, 0.5)
    w_value = gaussian(splits[5], (C, H * HD), C ** -0.5, 0.5)
    w_gate = gaussian(splits[6], (C, H * HD), C ** -0.5, 0.5)
    w_bias = draw_w_bias(jax.random.fold_in(splits[9], 71), 0)
    w_out = gaussian(splits[8], (H * HD, C), (H * HD) ** -0.5, 0.5)
    return dict(pair=pair, chain_ids=chain_ids, block_mask=block_mask, w_query=w_query, w_key=w_key, w_value=w_value, w_gate=w_gate, w_bias=w_bias, w_out=w_out)


masked_score = -1000000000.0
eps_norm = 1e-05

def layer_normed(values):
    wide = values.astype(jnp.float32)
    center = lax.optimization_barrier(jnp.mean(wide, axis=-1, keepdims=True))
    spread = lax.optimization_barrier(jnp.mean(jnp.square(wide - center), axis=-1, keepdims=True))
    return ((wide - center) * lax.rsqrt(spread + eps_norm)).astype(jnp.bfloat16)

def project_all(normed, weight):
    flat = normed.reshape(-1, normed.shape[-1])
    result = jnp.dot(flat, weight, preferred_element_type=jnp.float32)
    return result.reshape(normed.shape[0], normed.shape[1], weight.shape[1])

def reference(pair, chain_ids, block_mask, w_query, w_key, w_value, w_gate, w_bias, w_out):
    residues = pair.shape[0]
    head_count = w_bias.shape[1]
    feature_width = w_query.shape[1]
    head_dim = feature_width // head_count
    normed = layer_normed(pair)
    queries = project_all(normed, w_query).astype(jnp.bfloat16)
    key_all = project_all(normed, w_key).astype(jnp.bfloat16)
    value_all = project_all(normed, w_value).astype(jnp.bfloat16)
    bias_all = project_all(normed, w_bias).astype(jnp.bfloat16)
    queries, key_all, value_all, bias_all = lax.optimization_barrier((queries, key_all, value_all, bias_all))
    bias_heads = jnp.transpose(bias_all.astype(jnp.float32), (2, 0, 1))
    tile_of = jnp.arange(residues, dtype=jnp.int32) // TILE
    allowed = (block_mask[tile_of][:, tile_of] == 1) | (chain_ids[:, None] == chain_ids[None, :])
    group_size = 4

    def rows_block(offset):
        query_rows = lax.dynamic_slice_in_dim(queries, offset, group_size, 0).astype(jnp.float32)
        key_rows = lax.dynamic_slice_in_dim(key_all, offset, group_size, 0).astype(jnp.float32)
        value_rows = lax.dynamic_slice_in_dim(value_all, offset, group_size, 0).astype(jnp.float32)
        normed_rows = lax.dynamic_slice_in_dim(normed, offset, group_size, 0)
        allowed_rows = lax.dynamic_slice_in_dim(allowed, offset, group_size, 0)
        query_split = query_rows.reshape(group_size, residues, head_count, head_dim)
        key_split = key_rows.reshape(group_size, residues, head_count, head_dim)
        value_split = value_rows.reshape(group_size, residues, head_count, head_dim)
        scores = jnp.einsum('ijhd,ikhd->hijk', query_split, key_split)
        scores = scores * head_dim ** (-0.5) + bias_heads[:, None, :, :]
        scores = jnp.where(allowed_rows[None, :, None, :], scores, masked_score)
        top_score = lax.optimization_barrier(jnp.max(scores, axis=-1))
        expo = jnp.exp(scores - top_score[..., None])
        total_sum = lax.optimization_barrier(jnp.sum(expo, axis=-1))
        probs_low = lax.optimization_barrier(expo.astype(jnp.bfloat16))
        weighted = jnp.einsum('hijk,ikhd->ijhd', probs_low.astype(jnp.float32), value_split)
        attended = weighted / jnp.transpose(total_sum, (1, 2, 0))[..., None]
        attended = attended.reshape(group_size, residues, feature_width)
        flat_normed = normed_rows.reshape(-1, normed_rows.shape[-1])
        gate_rows = jax.nn.sigmoid(jnp.dot(flat_normed, w_gate, preferred_element_type=jnp.float32))
        gate_rows = gate_rows.reshape(group_size, residues, feature_width)
        return (gate_rows * attended).astype(jnp.bfloat16)
    offsets = jnp.arange(0, residues, group_size).astype(jnp.int32)
    gated = lax.map(rows_block, offsets).reshape(residues * residues, feature_width)
    update = jnp.dot(gated, w_out, preferred_element_type=jnp.float32).astype(jnp.bfloat16)
    update = update.reshape(residues, residues, w_out.shape[1])
    return jnp.transpose(update, (1, 0, 2)).reshape(N_COL, N_ROW, CPD, N, C)
```

```python
import functools
import math

import jax
import jax.numpy as jnp
from jax import lax
from jax.experimental import pallas as pl
from jax.experimental.pallas import tpu as pltpu
from jax.sharding import Mesh, PartitionSpec as P

ALL = ("xl", "z", "core", "xh", "y")
SIZES = (2, 4, 2, 2, 4)
LOG2E = math.log2(math.e)
SCALE = 32.0 ** -0.5
SAFE = 60.0
NT = (((1,), (1,)), ((), ()))
F32 = jnp.float32
BF16 = jnp.bfloat16


def dot(a, b):
    return jnp.dot(a, b, preferred_element_type=F32)


def dot_nt(a, b):
    return lax.dot_general(a, b, NT, preferred_element_type=F32)


def norm_kernel(pair_ref, wb_ref, normed_ref, bias_ref):
    rows = []
    for i in range(16):
        wide = pair_ref[i].astype(F32)
        center = jnp.mean(wide, axis=-1, keepdims=True)
        off = wide - center
        spread = jnp.mean(off * off, axis=-1, keepdims=True)
        normed = (off * lax.rsqrt(spread + 1e-5)).astype(BF16)
        normed_ref[i] = normed
        rows.append(dot_nt(wb_ref[...], normed))
    for h in range(4):
        bias_ref[h] = jnp.concatenate([r[h : h + 1] for r in rows], axis=0).astype(BF16)


def norm_and_bias(pair, wb):
    return pl.pallas_call(
        norm_kernel,
        grid=(4,),
        in_specs=[
            pl.BlockSpec((16, 128, 128), lambda g: (g, 0, 0)),
            pl.BlockSpec((16, 128), lambda g: (0, 0)),
        ],
        out_specs=[
            pl.BlockSpec((16, 128, 128), lambda g: (g, 0, 0)),
            pl.BlockSpec((4, 16, 128), lambda g: (0, g, 0)),
        ],
        out_shape=[
            jax.ShapeDtypeStruct((64, 128, 128), BF16),
            jax.ShapeDtypeStruct((4, 64, 128), BF16),
        ],
    )(pair, wb)


def attend_kernel(info, mask, x_ref, b0, b1, b2, b3, b4, b5, b6, b7, wq, wk, wv, wg, wo, out_ref,
                  bias_s, q_s, k_s, v_s, kb, vb, acc, top, even, bmax):
    t = pl.program_id(0)
    rows_all = q_s.shape[0]

    @pl.when(t == 0)
    def _():
        px, py, pz, core = info[2, 0], info[2, 1], info[2, 2], info[2, 3]
        biggest = jnp.zeros((8, 128), F32)
        for part, ref in enumerate((b0, b1, b2, b3, b4, b5, b6, b7)):
            cc = core if part < 4 else 1 - core
            p3 = part % 4

            def one(n, m, ref=ref, cc=cc, p3=p3):
                p2, p1 = n // 4, n % 4
                first = cc == 0
                x = px ^ jnp.where(first, p1, p3)
                y = py ^ jnp.where(first, p2, p1)
                z = pz ^ jnp.where(first, p3, p2)
                row = (x % 2) * 8 + z * 2 + cc
                col = (x // 2) * 4 + y
                wide = ref[n].astype(F32) * LOG2E
                bias_s[row * 8 + col] = wide
                return jnp.maximum(m, jnp.max(jnp.abs(wide).reshape(-1, 8, 128), axis=0))

            biggest = lax.fori_loop(0, 16, one, biggest)
        bmax[...] = biggest

    lane = lax.broadcasted_iota(jnp.int32, (128, 128), 1) // 32
    head_sum = (lax.broadcasted_iota(jnp.int32, (128, 128), 0) // 32 == lane).astype(BF16)
    q_top = jnp.zeros((8, 128), F32)
    k_top = jnp.zeros((8, 128), F32)
    for c in range(8):
        xt = x_ref[c, 0]
        rows = pl.ds(c * 128, 128)
        q = dot(xt, wq[...]).astype(BF16)
        k = dot(xt, wk[...]).astype(BF16)
        q_s[rows, :] = q
        k_s[rows, :] = k
        v_s[rows, :] = dot(xt, wv[...]).astype(BF16)
        q_top = jnp.maximum(q_top, jnp.max(dot(q * q, head_sum).reshape(16, 8, 128), axis=0))
        k_top = jnp.maximum(k_top, jnp.max(dot(k * k, head_sum).reshape(16, 8, 128), axis=0))
    q_top = jnp.max(q_top, axis=0, keepdims=True)
    k_top = jnp.max(k_top, axis=0, keepdims=True)
    reach = jnp.max(jnp.sqrt(q_top * k_top)) * (SCALE * 1.05) + jnp.max(bmax[...]) * (1.0 / LOG2E)
    safe = reach < SAFE

    acc[...] = jnp.zeros_like(acc)
    lo, hi = info[0, t], info[1, t]

    def pack_keys(kt):
        whole = mask[t, kt] == 1
        at = lax.broadcasted_iota(jnp.int32, (128, 128), 0) + kt * 128
        allowed = (at >= jnp.where(whole, 0, lo)) & (at < jnp.where(whole, 4096, hi))
        keys = k_s[pl.ds(pl.multiple_of(kt * 128, 128), 128), :].astype(F32)
        values = v_s[pl.ds(pl.multiple_of(kt * 128, 128), 128), :].astype(F32)
        for h in range(4):
            mine = lane == h
            kb[h * 128 : (h + 1) * 128, :] = jnp.where(mine, keys, 0.0).astype(BF16)
            vb[h * 128 : (h + 1) * 128, :128] = jnp.where(mine & allowed, values, 0.0).astype(BF16)
            vb[h * 128 : (h + 1) * 128, 128:] = jnp.where(mine & allowed, 1.0, 0.0).astype(BF16)

    def active(kt):
        return (mask[t, kt] == 1) | ((hi > kt * 128) & (lo < kt * 128 + 128))

    def scores_of(kt, start, count):
        s = dot_nt(q_s[pl.ds(start, count * 64), :], kb[...]).reshape(count, 64, 512)
        return [
            [s[n, :, h * 128 : (h + 1) * 128] * (SCALE * LOG2E) + bias_s[(start // 64 + n) * 8 + kt, h]
             for h in range(4)]
            for n in range(count)
        ]

    def join(blocks):
        return jnp.concatenate([jnp.concatenate(row, axis=1) for row in blocks], axis=0)

    @pl.when(safe)
    def _():
        def tile(kt, carry):
            @pl.when(active(kt))
            def _():
                pack_keys(kt)
                for start in range(0, rows_all, 512):
                    s = scores_of(kt, start, 8)
                    p = join([[jnp.exp2(a).astype(BF16) for a in row] for row in s])
                    acc[pl.ds(start, 512), :] += dot(p, vb[...])

            return carry

        lax.fori_loop(0, 8, tile, 0)

    @pl.when(jnp.logical_not(safe))
    def _():
        top[...] = jnp.full_like(top, -3e38)

        def first_pass(kt, carry):
            @pl.when(active(kt))
            def _():
                pack_keys(kt)
                whole = mask[t, kt] == 1
                at = lax.broadcasted_iota(jnp.int32, (64, 128), 1) + kt * 128
                allowed = (at >= jnp.where(whole, 0, lo)) & (at < jnp.where(whole, 4096, hi))

                def rows_of(g, carry):
                    start = pl.multiple_of(g * 64, 64)
                    s = scores_of(kt, start, 1)[0]
                    for h in range(4):
                        m = jnp.max(jnp.where(allowed, s[h], -3e38), axis=-1, keepdims=True)
                        old = top[h, pl.ds(start, 64), :]
                        top[h, pl.ds(start, 64), :] = jnp.maximum(old, jnp.broadcast_to(m, (64, 128)))
                    return carry

                lax.fori_loop(0, rows_all // 64, rows_of, 0)

            return carry

        lax.fori_loop(0, 8, first_pass, 0)

        def second_pass(kt, carry):
            @pl.when(active(kt))
            def _():
                pack_keys(kt)

                def rows_of(g, carry):
                    start = pl.multiple_of(g * 64, 64)
                    s = scores_of(kt, start, 1)[0]
                    p = [
                        jnp.exp2(jnp.minimum(s[h] - top[h, pl.ds(start, 64), :], 0.0)).astype(BF16)
                        for h in range(4)
                    ]
                    acc[pl.ds(start, 64), :] += dot(join([p]), vb[...])
                    return carry

                lax.fori_loop(0, rows_all // 64, rows_of, 0)

            return carry

        lax.fori_loop(0, 8, second_pass, 0)

    for c in range(rows_all // 128):
        rows = pl.ds(c * 128, 128)
        gate = 1.0 / (1.0 + jnp.exp2(dot(x_ref[c, 0], wg[...]) * -LOG2E))
        a = acc[rows, :]
        gated = (gate * (a[:, :128] / a[:, 128:])).astype(BF16)
        update = dot(gated, wo[...])

        @pl.when(t % 2 == 0)
        def _(update=update, rows=rows):
            even[rows, :] = update

        @pl.when(t % 2 == 1)
        def _(update=update, rows=rows, c=c):
            both = jnp.concatenate(
                [even[rows, :].reshape(16, 8, 128), update.reshape(16, 8, 128)], axis=1
            )
            out_ref[c * 16 : (c + 1) * 16, 0] = both.astype(BF16)


def attend(info, mask, x, bias_parts, weights):
    smem = pl.BlockSpec(memory_space=pltpu.SMEM)
    vmem = pl.BlockSpec(memory_space=pltpu.VMEM)
    return pl.pallas_call(
        attend_kernel,
        grid=(8,),
        in_specs=[smem, smem, pl.BlockSpec((8, 1, 128, 128), lambda t: (0, t, 0, 0))] + [vmem] * 13,
        out_specs=pl.BlockSpec((128, 1, 16, 128), lambda t: (0, t // 2, 0, 0)),
        out_shape=jax.ShapeDtypeStruct((128, 4, 16, 128), BF16),
        scratch_shapes=[
            pltpu.VMEM((128, 4, 64, 128), F32),
            pltpu.VMEM((1024, 128), BF16),
            pltpu.VMEM((1024, 128), BF16),
            pltpu.VMEM((1024, 128), BF16),
            pltpu.VMEM((512, 128), BF16),
            pltpu.VMEM((512, 256), BF16),
            pltpu.VMEM((1024, 256), F32),
            pltpu.VMEM((4, 1024, 128), F32),
            pltpu.VMEM((1024, 128), F32),
            pltpu.VMEM((8, 128), F32),
        ],
        compiler_params=pltpu.CompilerParams(vmem_limit_bytes=56 * 2**20),
    )(info, mask, x, *bias_parts, *weights)


def order_kernel(in_ref, out_ref, wide):
    wide[...] = in_ref[...].reshape(8192, 128).astype(F32)
    for s in range(8):
        for t in range(8):
            for core in range(2):
                start = core * 64 + t * 8 + s
                got = wide[pl.ds(start, 64, stride=128), :]
                out_ref[s, pl.ds(t * 128 + core * 64, 64), :] = got.astype(BF16)


def put_in_order(received):
    vmem = pl.BlockSpec(memory_space=pltpu.VMEM)
    return pl.pallas_call(
        order_kernel,
        in_specs=[vmem],
        out_specs=vmem,
        out_shape=jax.ShapeDtypeStruct((8, 1024, 128), BF16),
        scratch_shapes=[pltpu.VMEM((8192, 128), F32)],
        compiler_params=pltpu.CompilerParams(vmem_limit_bytes=32 * 2**20),
    )(received)


def index_of(xl, z, core, xh, y):
    return (((xl * 4 + z) * 2 + core) * 2 + xh) * 4 + y


def partners(orders, stage, flip):
    pairs = []
    for xl in range(2):
        for z in range(4):
            for core in range(2):
                for xh in range(2):
                    for y in range(4):
                        place = {"x": xh * 2 + xl, "y": y, "z": z}
                        place[orders[core][stage]] ^= flip
                        to = index_of(place["x"] % 2, place["z"], core, place["x"] // 2, place["y"])
                        pairs.append((index_of(xl, z, core, xh, y), to))
    return pairs


def gather_bias(bias):
    orders = (("x", "y", "z"), ("y", "z", "x"))
    held = bias[None]
    for stage in range(2):
        parts = [held] + [lax.ppermute(held, ALL, partners(orders, stage, flip)) for flip in (1, 2, 3)]
        held = jnp.concatenate(parts, axis=0)
    parts = [held] + [lax.ppermute(held, ALL, partners(orders, 2, flip)) for flip in (1, 2, 3)]
    return parts + [lax.ppermute(p, "core", [(0, 1), (1, 0)]) for p in parts]


def body(pair, chain_ids, block_mask, w_query, w_key, w_value, w_gate, w_bias, w_out):
    at = {name: lax.axis_index(name) for name in ALL}
    column = at["core"] * 64 + lax.axis_index(("xh", "y", "xl", "z"))
    mine = lax.dynamic_slice_in_dim(chain_ids.reshape(8, 128), column, 1, 1)
    lo = jnp.sum((chain_ids[None, :] < mine).astype(jnp.int32), axis=1)
    hi = jnp.sum((chain_ids[None, :] <= mine).astype(jnp.int32), axis=1)
    place = jnp.stack([at["xh"] * 2 + at["xl"], at["y"], at["z"], at["core"]] + [at["z"] * 0] * 4)
    info = jnp.stack([lo, hi, place]).astype(jnp.int32)
    wb = jnp.pad(w_bias.T, ((0, 12), (0, 0)))
    normed, bias = norm_and_bias(pair, wb)
    bias_parts = gather_bias(bias)
    x = lax.all_to_all(normed, ("xh", "y", "xl", "z"), split_axis=0, concat_axis=0, tiled=True)
    update = attend(info, block_mask, x.reshape(8, 8, 128, 128), bias_parts,
                    (w_query, w_key, w_value, w_gate, w_out))
    back = lax.all_to_all(update, ("xh", "y", "xl", "z", "core"), split_axis=0, concat_axis=0, tiled=True)
    return put_in_order(back).reshape(1, 1, 8, 1024, 128)


def solution(mesh):
    fine = Mesh(mesh.devices.reshape(SIZES), ALL)
    row, col = ("xl", "z", "core"), ("xh", "y")
    return jax.shard_map(
        body,
        mesh=fine,
        in_specs=(P(row, col, None), P(), P(), P(), P(), P(), P(), P(), P()),
        out_specs=P(col, row, None, None, None),
        check_vma=False,
    )
```

```python
import functools
import math

import jax
import jax.numpy as jnp
from jax import lax
from jax.experimental import pallas as pl
from jax.experimental.pallas import tpu as pltpu
from jax.sharding import Mesh, PartitionSpec as P

ALL = ("xl", "z", "core", "xh", "y")
SIZES = (2, 4, 2, 2, 4)
LOG2E = math.log2(math.e)
SCALE = 32.0 ** -0.5
LEAST = 1e-25
MOST = 1e30
NT = (((1,), (1,)), ((), ()))
F32 = jnp.float32
BF16 = jnp.bfloat16


def dot(a, b):
    return jnp.dot(a, b, preferred_element_type=F32)


def dot_nt(a, b):
    return lax.dot_general(a, b, NT, preferred_element_type=F32)


def layer_normed(narrow):
    wide = narrow.astype(F32)
    center = jnp.mean(wide, axis=-1, keepdims=True)
    off = wide - center
    spread = jnp.mean(off * off, axis=-1, keepdims=True)
    normed = (off * lax.rsqrt(spread + 1e-5)).reshape(16, 8, 128)
    return jnp.concatenate(
        [normed[:, :4].reshape(64, 128), normed[:, 4:].reshape(64, 128)], axis=0
    ).astype(BF16)


def bias_kernel(pair_ref, wb_ref, bias_ref):
    rows = [dot_nt(wb_ref[...], layer_normed(pair_ref[i])) for i in range(32)]
    for half in range(2):
        for h in range(4):
            picked = [rows[i][h : h + 1] for i in range(32) if (i % 8) // 4 == half]
            bias_ref[half, 0, h] = jnp.concatenate(picked, axis=0).astype(BF16)


def bias_of(pair, wb):
    return pl.pallas_call(
        bias_kernel,
        grid=(2,),
        in_specs=[
            pl.BlockSpec((32, 128, 128), lambda g: (g, 0, 0)),
            pl.BlockSpec((16, 128), lambda g: (0, 0)),
        ],
        out_specs=pl.BlockSpec((2, 1, 4, 16, 128), lambda g: (0, 0, 0, g, 0)),
        out_shape=jax.ShapeDtypeStruct((2, 1, 4, 32, 128), BF16),
    )(pair, wb)


def norm_kernel(x_ref, normed_ref):
    for i in range(16):
        normed_ref[i] = layer_normed(x_ref[i])


def norm_rows(x):
    block = pl.BlockSpec((16, 128, 128), lambda g: (g, 0, 0))
    return pl.pallas_call(
        norm_kernel,
        grid=(4,),
        in_specs=[block],
        out_specs=block,
        out_shape=jax.ShapeDtypeStruct((64, 128, 128), BF16),
        cost_estimate=pl.CostEstimate(flops=10**8, bytes_accessed=20 * 2**20, transcendentals=0),
    )(x)


def tile_in_use(info, mask, t, kt):
    return (mask[t, kt] == 1) | ((info[1, t] > kt * 128) & (info[0, t] < kt * 128 + 128))


def attend_kernel(half, info, mask, x_ref, wq, wk, wv, wg, wo, a0, a1, a2, a3, a4, a5, a6, a7,
                  out_ref, tiles, w_s, q_ref, k_ref, v_ref, gates, bias_s, kb0, kb1, vb0, vb1, p0, p1, acc, top, wide, sems):
    copies = [
        pltpu.make_async_copy(ref, bias_s.at[pl.ds(n * 16, 16)], sems.at[n])
        for n, ref in enumerate((a0, a1, a2, a3, a4, a5, a6, a7))
    ]
    for copy in copies:
        copy.start()
    px, py, pz, core = info[2, 0], info[2, 1], info[2, 2], info[2, 3]
    here = (core * 64 + pz * 16 + py * 4 + px, (1 - core) * 64 + px * 16 + pz * 4 + py)
    lane = lax.broadcasted_iota(jnp.int32, (128, 128), 1) // 32
    spot = lax.broadcasted_iota(jnp.int32, (128, 128), 0)
    spot = (spot % 64) // 4 * 8 + spot // 64 * 4 + spot % 4
    spot_lanes = lax.broadcasted_iota(jnp.int32, (64, 128), 1)
    spot_lanes = (spot_lanes % 64) // 4 * 8 + spot_lanes // 64 * 4 + spot_lanes % 4

    def add(e, n):
        tiles[n] = e
        return n + tile_in_use(info, mask, e // 8, e % 8).astype(jnp.int32)

    count = lax.fori_loop(0, 64, add, 0)
    tiles[count] = -1
    tiles[count + 1] = -1

    w_s[0] = jnp.concatenate([wk[...], wv[...]], axis=1)
    w_s[1] = jnp.concatenate([wq[...], wg[...]], axis=1)

    def project(t, carry):
        both = dot(x_ref[:, t].reshape(1024, 128), w_s[0]).astype(BF16)
        k_ref[t] = both[:, :128]
        v_ref[t] = both[:, 128:]
        both = dot(x_ref[:, t, half].reshape(512, 128), w_s[1])
        q_ref[0, t] = both[:, :128].astype(BF16)
        gates[t] = 1.0 / (1.0 + jnp.exp2(both[:, 128:] * -LOG2E))
        acc[t] = jnp.zeros((512, 256), F32)
        return carry

    lax.fori_loop(0, 8, project, 0)

    def bounds(t, kt, valid):
        whole = (mask[t, kt] == 1) & valid
        lo = jnp.where(valid, jnp.where(whole, 0, info[0, t]), 5000)
        hi = jnp.where(valid, jnp.where(whole, 5000, info[1, t]), 0)
        return lo - kt * 128, hi - kt * 128

    def entry(n):
        e = tiles[n]
        held = jnp.maximum(e, 0)
        return held // 8, held % 8, e >= 0

    def block(ref, t, kt):
        return ref[t, pl.ds(pl.multiple_of(kt * 128, 128), 128), :]

    def pack_keys(t, kt, kb):
        keys = block(k_ref, t, kt)
        for h in range(4):
            kb[h * 128 : (h + 1) * 128, :] = jnp.where(lane == h, keys, jnp.zeros_like(keys))

    def pack_values(t, kt, valid, vb):
        lo, hi = bounds(t, kt, valid)
        allowed = (spot >= lo) & (spot < hi)
        values = block(v_ref, t, kt).astype(F32)
        for h in range(4):
            mine = (lane == h) & allowed
            vb[h * 128 : (h + 1) * 128, :128] = jnp.where(mine, values, 0.0).astype(BF16)
            vb[h * 128 : (h + 1) * 128, 128:] = jnp.where(mine, 1.0, 0.0).astype(BF16)

    def bias_tiles(g, kt):
        xl, z = g // 4, g % 4
        xh, y = kt // 4, kt % 4
        at0 = here[0] ^ (z * 16 + xl) ^ (y * 4 + xh * 2)
        at1 = here[1] ^ (xl * 16 + z * 4) ^ (xh * 32 + y)
        return at0, at1

    def scores(s, at, h):
        return (s * SCALE + bias_s[at, h].astype(F32)) * LOG2E

    def weigh(t, kt, kb, p):
        s = dot_nt(q_ref[0, t], kb[...])
        for g in range(8):
            for part, at in enumerate(bias_tiles(g, kt)):
                start = g * 64 + part * 32
                for h in range(4):
                    z = scores(s[start : start + 32, h * 128 : (h + 1) * 128], at, h)
                    p[start : start + 32, h * 128 : (h + 1) * 128] = jnp.exp2(z).astype(BF16)

    def mix(t, vb, p):
        acc[t] += dot(p[...], vb[...])

    p1[...] = jnp.zeros_like(p1)
    vb1[...] = jnp.zeros_like(vb1)
    t, kt, _ = entry(0)
    pack_keys(t, kt, kb0)
    for copy in copies:
        copy.wait()

    def two(m, carry):
        t0, kt0, valid0 = entry(2 * m)
        t1, kt1, valid1 = entry(2 * m + 1)
        t2, kt2, _ = entry(jnp.minimum(2 * m + 2, count))
        before, _, _ = entry(jnp.maximum(2 * m - 1, 0))
        weigh(t0, kt0, kb0, p0)
        mix(before, vb1, p1)
        pack_values(t0, kt0, valid0, vb0)
        pack_keys(t1, kt1, kb1)
        weigh(t1, kt1, kb1, p1)
        mix(t0, vb0, p0)
        pack_values(t1, kt1, valid1, vb1)
        pack_keys(t2, kt2, kb0)
        return carry

    pairs = (count + 1) // 2
    lax.fori_loop(0, pairs, two, 0)
    last, _, _ = entry(2 * pairs - 1)
    mix(last, vb1, p1)

    def redo(t):
        top[...] = jnp.full_like(top, -3e38)
        acc[t] = jnp.zeros((512, 256), F32)

        def per_tile(body):
            def step(kt, carry):
                @pl.when(tile_in_use(info, mask, t, kt))
                def _():
                    pack_keys(t, kt, kb0)
                    pack_values(t, kt, True, vb0)

                    def rows(g, carry):
                        start = pl.multiple_of(g * 64, 64)
                        s = dot_nt(q_ref[0, t, pl.ds(start, 64), :], kb0[...])
                        ats = bias_tiles(g, kt)
                        z = [
                            jnp.concatenate(
                                [scores(s[i * 32 : i * 32 + 32, h * 128 : (h + 1) * 128], ats[i], h) for i in range(2)],
                                axis=0,
                            )
                            for h in range(4)
                        ]
                        body(kt, start, z)
                        return carry

                    lax.fori_loop(0, 8, rows, 0)

                return carry

            lax.fori_loop(0, 8, step, 0)

        def find_top(kt, start, z):
            lo, hi = bounds(t, kt, True)
            allowed = (spot_lanes >= lo) & (spot_lanes < hi)
            for h in range(4):
                m = jnp.max(jnp.where(allowed, z[h], -3e38), axis=-1, keepdims=True)
                old = top[h, pl.ds(start, 64), :]
                top[h, pl.ds(start, 64), :] = jnp.maximum(old, jnp.broadcast_to(m, (64, 128)))

        def add_up(kt, start, z):
            p = [jnp.exp2(jnp.minimum(z[h] - top[h, pl.ds(start, 64), :], 0.0)) for h in range(4)]
            p = jnp.concatenate(p, axis=1).astype(BF16)
            acc[t, pl.ds(start, 64), :] += dot(p, vb0[...])

        per_tile(find_top)
        per_tile(add_up)

    def check(t, carry):
        total = acc[t, :, 128:]
        good = (total > LEAST) & (total < MOST)
        fine = jnp.min(jnp.where(good, 1.0, 0.0))

        @pl.when(fine < 0.5)
        def _():
            redo(t)

        return carry

    lax.fori_loop(0, 8, check, 0)
    for t in range(8):
        a = acc[t]
        gated = (gates[t] * (a[:, :128] / a[:, 128:])).astype(BF16)
        wide[:, t * 4 : t * 4 + 4, :] = dot(gated, wo[...]).reshape(128, 4, 128)
    out_ref[...] = wide[...].astype(BF16)


def attend(half, info, mask, x, weights, bias_parts):
    smem = pl.BlockSpec(memory_space=pltpu.SMEM)
    vmem = pl.BlockSpec(memory_space=pltpu.VMEM)
    hbm = pl.BlockSpec(memory_space=pl.ANY)
    return pl.pallas_call(
        functools.partial(attend_kernel, half),
        in_specs=[smem, smem] + [vmem] * 6 + [hbm] * 8,
        out_specs=vmem,
        out_shape=jax.ShapeDtypeStruct((128, 32, 128), BF16),
        scratch_shapes=[
            pltpu.SMEM((72,), jnp.int32),
            pltpu.VMEM((2, 128, 256), BF16),
            pltpu.VMEM((1, 8, 512, 128), BF16),
            pltpu.VMEM((8, 1024, 128), BF16),
            pltpu.VMEM((8, 1024, 128), BF16),
            pltpu.VMEM((8, 512, 128), F32),
            pltpu.VMEM((128, 4, 32, 128), BF16),
            pltpu.VMEM((512, 128), BF16),
            pltpu.VMEM((512, 128), BF16),
            pltpu.VMEM((512, 256), BF16),
            pltpu.VMEM((512, 256), BF16),
            pltpu.VMEM((512, 512), BF16),
            pltpu.VMEM((512, 512), BF16),
            pltpu.VMEM((8, 512, 256), F32),
            pltpu.VMEM((4, 512, 128), F32),
            pltpu.VMEM((128, 32, 128), F32),
            pltpu.SemaphoreType.DMA((8,)),
        ],
        compiler_params=pltpu.CompilerParams(vmem_limit_bytes=60 * 2**20),
        cost_estimate=pl.CostEstimate(flops=20 * 10**9, bytes_accessed=12 * 2**20, transcendentals=11 * 10**6),
    )(info, mask, x, *weights, *bias_parts)


def order_kernel(in_ref, *refs):
    out_ref, wide = refs[-2:]
    wide[...] = in_ref[...].reshape(4096, 128).astype(F32)
    for s in range(4):
        for t in range(8):
            for core in range(2):
                got = wide[pl.ds(core * 32 + t * 4 + s, 64, stride=64), :]
                out_ref[s, pl.ds(t * 128 + core * 64, 64), :] = got.astype(BF16)


def put_in_order(half, received, before):
    vmem = pl.BlockSpec(memory_space=pltpu.VMEM)
    args = [received] if before is None else [received, before]
    return pl.pallas_call(
        order_kernel,
        grid=(1,),
        in_specs=[vmem] + [pl.BlockSpec(memory_space=pl.ANY)] * (len(args) - 1),
        out_specs=pl.BlockSpec((4, 1024, 128), lambda g: (half, 0, 0)),
        out_shape=jax.ShapeDtypeStruct((8, 1024, 128), BF16),
        input_output_aliases={} if before is None else {1: 0},
        scratch_shapes=[pltpu.VMEM((4096, 128), F32)],
        compiler_params=pltpu.CompilerParams(vmem_limit_bytes=32 * 2**20),
    )(*args)


def index_of(xl, z, core, xh, y):
    return (((xl * 4 + z) * 2 + core) * 2 + xh) * 4 + y


def partners(orders, flips):
    pairs = []
    for xl in range(2):
        for z in range(4):
            for core in range(2):
                for xh in range(2):
                    for y in range(4):
                        place = {"x": xh * 2 + xl, "y": y, "z": z}
                        for axis, flip in zip(orders[core], flips):
                            place[axis] ^= flip
                        to = index_of(place["x"] % 2, place["z"], core, place["x"] // 2, place["y"])
                        pairs.append((index_of(xl, z, core, xh, y), to))
    return pairs


ORDERS = (("x", "y", "z"), ("y", "z", "x"))


def from_partners(held, flips):
    return lax.ppermute(held, ALL, partners(ORDERS, flips))


def from_line(held):
    return [from_partners(held, (0, 0, flip)) for flip in (1, 2, 3)]


def other_core(held):
    return lax.ppermute(held, "core", [(0, 1), (1, 0)])


def body(pair, chain_ids, block_mask, w_query, w_key, w_value, w_gate, w_bias, w_out):
    at = {name: lax.axis_index(name) for name in ALL}
    column = at["core"] * 64 + lax.axis_index(("xh", "y", "xl", "z"))
    mine = lax.dynamic_slice_in_dim(chain_ids.reshape(8, 128), column, 1, 1)
    lo = jnp.sum((chain_ids[None, :] < mine).astype(jnp.int32), axis=1)
    hi = jnp.sum((chain_ids[None, :] <= mine).astype(jnp.int32), axis=1)
    place = jnp.stack([at["xh"] * 2 + at["xl"], at["y"], at["z"], at["core"]] + [at["z"] * 0] * 4)
    info = jnp.stack([lo, hi, place]).astype(jnp.int32)
    bias = bias_of(pair, jnp.pad(w_bias.T, ((0, 12), (0, 0))))
    x = lax.all_to_all(pair, ("xh", "y", "xl", "z"), split_axis=0, concat_axis=0, tiled=True)
    held = jnp.concatenate([bias] + [from_partners(bias, (n, 0, 0)) for n in (1, 2, 3)], axis=1)
    held, x = lax.optimization_barrier((held, x))
    pieces = [held] + [from_partners(held, (0, n, 0)) for n in (1, 2, 3)]
    halves = [jnp.concatenate([p[n] for p in pieces], axis=0) for n in range(2)]
    x = norm_rows(x)
    halves[0], x = lax.optimization_barrier((halves[0], x))
    parts = [halves[0]] + from_line(halves[0])
    *parts, later = lax.optimization_barrier((*parts, halves[1]))
    first = parts + [other_core(p) for p in parts]
    second = [later] + from_line(later)
    x = x.reshape(8, 8, 2, 64, 128)
    weights = (w_query, w_key, w_value, w_gate, w_out)
    done = None
    backs = []
    for n in range(2):
        if n == 1:
            update, *second = lax.optimization_barrier((update, *second))
            backs.append(lax.all_to_all(update, ("xh", "y", "xl", "z", "core"), split_axis=0, concat_axis=0, tiled=True))
            second = second + [other_core(p) for p in second]
        update = attend(n, info, block_mask, x, weights, second if n else first)
    backs.append(lax.all_to_all(update, ("xh", "y", "xl", "z", "core"), split_axis=0, concat_axis=0, tiled=True))
    for n in range(2):
        done = put_in_order(n, backs[n], done)
    return done.reshape(1, 1, 8, 1024, 128)


def solution(mesh):
    fine = Mesh(mesh.devices.reshape(SIZES), ALL)
    row, col = ("xl", "z", "core"), ("xh", "y")
    return jax.shard_map(
        body,
        mesh=fine,
        in_specs=(P(row, col, None), P(), P(), P(), P(), P(), P(), P(), P()),
        out_specs=P(col, row, None, None, None),
        check_vma=False,
    )
```

```python
import functools
import math

import jax
import jax.numpy as jnp
from jax import lax
from jax.experimental import pallas as pl
from jax.experimental.pallas import tpu as pltpu
from jax.sharding import Mesh, PartitionSpec as P

ALL = ("xl", "z", "core", "xh", "y")
SIZES = (2, 4, 2, 2, 4)
LOG2E = math.log2(math.e)
SCALE = 32.0 ** -0.5
LEAST = 1e-25
MOST = 1e30
NT = (((1,), (1,)), ((), ()))
F32 = jnp.float32
BF16 = jnp.bfloat16


def dot(a, b):
    return jnp.dot(a, b, preferred_element_type=F32)


def dot_nt(a, b):
    return lax.dot_general(a, b, NT, preferred_element_type=F32)


def layer_normed(narrow):
    wide = narrow.astype(F32)
    center = jnp.mean(wide, axis=-1, keepdims=True)
    off = wide - center
    spread = jnp.mean(off * off, axis=-1, keepdims=True)
    normed = (off * lax.rsqrt(spread + 1e-5)).reshape(16, 8, 128)
    return jnp.concatenate(
        [normed[:, :4].reshape(64, 128), normed[:, 4:].reshape(64, 128)], axis=0
    ).astype(BF16)


def bias_kernel(pair_ref, wb_ref, bias_ref):
    rows = [dot_nt(wb_ref[...], layer_normed(pair_ref[i])) for i in range(32)]
    for half in range(2):
        for h in range(4):
            picked = [rows[i][h : h + 1] for i in range(32) if (i % 8) // 4 == half]
            bias_ref[half, 0, h] = jnp.concatenate(picked, axis=0).astype(BF16)


def bias_of(pair, wb):
    return pl.pallas_call(
        bias_kernel,
        grid=(2,),
        in_specs=[
            pl.BlockSpec((32, 128, 128), lambda g: (g, 0, 0)),
            pl.BlockSpec((16, 128), lambda g: (0, 0)),
        ],
        out_specs=pl.BlockSpec((2, 1, 4, 16, 128), lambda g: (0, 0, 0, g, 0)),
        out_shape=jax.ShapeDtypeStruct((2, 1, 4, 32, 128), BF16),
    )(pair, wb)


def norm_kernel(x_ref, normed_ref):
    ones = jnp.ones((384, 128), BF16)
    for i in range(0, 16, 8):
        narrow = x_ref[i : i + 8].reshape(1024, 128)
        off = narrow.astype(F32) - dot(narrow, ones[:128]) * (1.0 / 128)
        left = off * off
        terms = []
        for _ in range(3):
            terms.append(left.astype(BF16))
            left = left - terms[-1].astype(F32)
        spread = dot(jnp.concatenate(terms, axis=1), ones) * (1.0 / 128)
        normed = (off * lax.rsqrt(spread + 1e-5)).reshape(8, 16, 8, 128)
        normed_ref[i : i + 8] = jnp.concatenate(
            [normed[:, :, :4].reshape(8, 64, 128), normed[:, :, 4:].reshape(8, 64, 128)], axis=1
        ).astype(BF16)


def norm_rows(x):
    block = pl.BlockSpec((16, 128, 128), lambda g: (g, 0, 0))
    return pl.pallas_call(
        norm_kernel,
        grid=(4,),
        in_specs=[block],
        out_specs=block,
        out_shape=jax.ShapeDtypeStruct((64, 128, 128), BF16),
        cost_estimate=pl.CostEstimate(flops=10**8, bytes_accessed=20 * 2**20, transcendentals=0),
    )(x)


def tile_in_use(info, mask, t, kt):
    return (mask[t, kt] == 1) | ((info[1, t] > kt * 128) & (info[0, t] < kt * 128 + 128))


def attend_kernel(half, info, mask, x_ref, wq, wk, wv, wg, wo, a0, a1, a2, a3, a4, a5, a6, a7,
                  out_ref, tiles, w_s, q_ref, k_ref, v_ref, gates, bias_s, kb0, kb1, vb0, vb1, p0, p1, acc, top, wide, sems):
    copies = [
        pltpu.make_async_copy(ref, bias_s.at[pl.ds(n * 16, 16)], sems.at[n])
        for n, ref in enumerate((a0, a1, a2, a3, a4, a5, a6, a7))
    ]
    for copy in copies:
        copy.start()
    px, py, pz, core = info[2, 0], info[2, 1], info[2, 2], info[2, 3]
    here = (core * 64 + pz * 16 + py * 4 + px, (1 - core) * 64 + px * 16 + pz * 4 + py)
    lane = lax.broadcasted_iota(jnp.int32, (128, 128), 1) // 32
    spot = lax.broadcasted_iota(jnp.int32, (128, 128), 0)
    spot = (spot % 64) // 4 * 8 + spot // 64 * 4 + spot % 4
    spot_lanes = lax.broadcasted_iota(jnp.int32, (32, 128), 1)
    spot_lanes = (spot_lanes % 64) // 4 * 8 + spot_lanes // 64 * 4 + spot_lanes % 4

    def add(e, n):
        tiles[n] = e
        return n + tile_in_use(info, mask, e // 8, e % 8).astype(jnp.int32)

    count = lax.fori_loop(0, 64, add, 0)
    tiles[count] = -1
    tiles[count + 1] = -1

    w_s[0] = jnp.concatenate([wk[...], wv[...]], axis=1)
    w_s[1] = jnp.concatenate([wq[...], wg[...]], axis=1)

    def project(t, carry):
        both = dot(x_ref[:, t].reshape(1024, 128), w_s[0]).astype(BF16)
        k_ref[t] = both[:, :128]
        v_ref[t] = both[:, 128:]
        both = dot(x_ref[:, t, half].reshape(512, 128), w_s[1])
        q_ref[0, t] = both[:, :128].astype(BF16)
        gates[t] = 1.0 / (1.0 + jnp.exp2(both[:, 128:] * -LOG2E))
        acc[t] = jnp.zeros((512, 256), F32)
        return carry

    lax.fori_loop(0, 8, project, 0)

    def bounds(t, kt, valid):
        whole = (mask[t, kt] == 1) & valid
        lo = jnp.where(valid, jnp.where(whole, 0, info[0, t]), 5000)
        hi = jnp.where(valid, jnp.where(whole, 5000, info[1, t]), 0)
        return lo - kt * 128, hi - kt * 128

    def entry(n):
        e = tiles[n]
        held = jnp.maximum(e, 0)
        return held // 8, held % 8, e >= 0

    def block(ref, t, kt):
        return ref[t, pl.ds(pl.multiple_of(kt * 128, 128), 128), :]

    def pack_keys(t, kt, kb):
        keys = block(k_ref, t, kt)
        for h in range(4):
            kb[h * 128 : (h + 1) * 128, :] = jnp.where(lane == h, keys, jnp.zeros_like(keys))

    def pack_values(t, kt, valid, vb):
        lo, hi = bounds(t, kt, valid)
        allowed = (spot >= lo) & (spot < hi)
        values = block(v_ref, t, kt).astype(F32)
        for h in range(4):
            mine = (lane == h) & allowed
            vb[h * 128 : (h + 1) * 128, :128] = jnp.where(mine, values, 0.0).astype(BF16)
            vb[h * 128 : (h + 1) * 128, 128:] = jnp.where(mine, 1.0, 0.0).astype(BF16)

    def bias_tiles(g, kt):
        xl, z = g // 4, g % 4
        xh, y = kt // 4, kt % 4
        at0 = here[0] ^ (z * 16 + xl) ^ (y * 4 + xh * 2)
        at1 = here[1] ^ (xl * 16 + z * 4) ^ (xh * 32 + y)
        return at0, at1

    def scores(s, at, h):
        return (s * SCALE + bias_s[at, h].astype(F32)) * LOG2E

    def scored(t, kt, kb, use):
        s = dot_nt(q_ref[0, t], kb[...])
        for g in range(8):
            for part, at in enumerate(bias_tiles(g, kt)):
                start = g * 64 + part * 32
                for h in range(4):
                    z = scores(s[start : start + 32, h * 128 : (h + 1) * 128], at, h)
                    use(slice(start, start + 32), h, z)

    def weigh(t, kt, kb, p):
        def seen(rows, h, z):
            p[rows, h * 128 : (h + 1) * 128] = jnp.exp2(z).astype(BF16)

        scored(t, kt, kb, seen)

    def mix(t, vb, p):
        acc[t] += dot(p[...], vb[...])

    p1[...] = jnp.zeros_like(p1)
    vb1[...] = jnp.zeros_like(vb1)
    t, kt, _ = entry(0)
    pack_keys(t, kt, kb0)
    for copy in copies:
        copy.wait()

    def two(m, carry):
        t0, kt0, valid0 = entry(2 * m)
        t1, kt1, valid1 = entry(2 * m + 1)
        t2, kt2, _ = entry(jnp.minimum(2 * m + 2, count))
        before, _, _ = entry(jnp.maximum(2 * m - 1, 0))
        mix(before, vb1, p1)
        weigh(t0, kt0, kb0, p0)
        pack_values(t0, kt0, valid0, vb0)
        pack_keys(t1, kt1, kb1)
        mix(t0, vb0, p0)
        weigh(t1, kt1, kb1, p1)
        pack_values(t1, kt1, valid1, vb1)
        pack_keys(t2, kt2, kb0)
        return carry

    pairs = (count + 1) // 2
    lax.fori_loop(0, pairs, two, 0)
    last, _, _ = entry(2 * pairs - 1)
    mix(last, vb1, p1)

    def redo(t):
        top[...] = jnp.full_like(top, -3e38)
        acc[t] = jnp.zeros((512, 256), F32)

        def per_tile(body):
            def step(kt, carry):
                @pl.when(tile_in_use(info, mask, t, kt))
                def _():
                    pack_keys(t, kt, kb0)
                    pack_values(t, kt, True, vb0)
                    body(kt)

                return carry

            lax.fori_loop(0, 8, step, 0)

        def find_top(kt):
            lo, hi = bounds(t, kt, True)
            allowed = (spot_lanes >= lo) & (spot_lanes < hi)

            def seen(rows, h, z):
                top[h, rows, :] = jnp.maximum(top[h, rows, :], jnp.where(allowed, z, -3e38))

            scored(t, kt, kb0, seen)

        def add_up(kt):
            def seen(rows, h, z):
                p = jnp.exp2(jnp.minimum(z - top[h, rows, :], 0.0))
                p0[rows, h * 128 : (h + 1) * 128] = p.astype(BF16)

            scored(t, kt, kb0, seen)
            mix(t, vb0, p0)

        per_tile(find_top)
        for h in range(4):
            top[h] = jnp.broadcast_to(jnp.max(top[h], axis=-1, keepdims=True), (512, 128))
        per_tile(add_up)

    def worst(t):
        total = acc[t, :, 128:]
        bad = jnp.where((total > LEAST) & (total < MOST), 0.0, 1.0)
        return jnp.max(bad.reshape(64, 8, 128), axis=0)

    def check(t, carry):
        @pl.when(jnp.max(worst(t)) > 0.5)
        def _():
            redo(t)

        return carry

    any_bad = lax.fori_loop(0, 8, lambda t, m: jnp.maximum(m, worst(t)), jnp.zeros((8, 128), F32))

    @pl.when(jnp.max(any_bad) > 0.5)
    def _():
        lax.fori_loop(0, 8, check, 0)

    for t in range(8):
        a = acc[t]
        gated = (gates[t] * (a[:, :128] / a[:, 128:])).astype(BF16)
        wide[:, t * 4 : t * 4 + 4, :] = dot(gated, wo[...]).reshape(128, 4, 128)
    out_ref[...] = wide[...].astype(BF16)


def attend(half, info, mask, x, weights, bias_parts):
    smem = pl.BlockSpec(memory_space=pltpu.SMEM)
    vmem = pl.BlockSpec(memory_space=pltpu.VMEM)
    hbm = pl.BlockSpec(memory_space=pl.ANY)
    return pl.pallas_call(
        functools.partial(attend_kernel, half),
        in_specs=[smem, smem] + [vmem] * 6 + [hbm] * 8,
        out_specs=vmem,
        out_shape=jax.ShapeDtypeStruct((128, 32, 128), BF16),
        scratch_shapes=[
            pltpu.SMEM((72,), jnp.int32),
            pltpu.VMEM((2, 128, 256), BF16),
            pltpu.VMEM((1, 8, 512, 128), BF16),
            pltpu.VMEM((8, 1024, 128), BF16),
            pltpu.VMEM((8, 1024, 128), BF16),
            pltpu.VMEM((8, 512, 128), F32),
            pltpu.VMEM((128, 4, 32, 128), BF16),
            pltpu.VMEM((512, 128), BF16),
            pltpu.VMEM((512, 128), BF16),
            pltpu.VMEM((512, 256), BF16),
            pltpu.VMEM((512, 256), BF16),
            pltpu.VMEM((512, 512), BF16),
            pltpu.VMEM((512, 512), BF16),
            pltpu.VMEM((8, 512, 256), F32),
            pltpu.VMEM((4, 512, 128), F32),
            pltpu.VMEM((128, 32, 128), F32),
            pltpu.SemaphoreType.DMA((8,)),
        ],
        compiler_params=pltpu.CompilerParams(vmem_limit_bytes=60 * 2**20),
        cost_estimate=pl.CostEstimate(flops=20 * 10**9, bytes_accessed=12 * 2**20, transcendentals=11 * 10**6),
    )(info, mask, x, *weights, *bias_parts)


def order_kernel(in_ref, *refs):
    out_ref, wide = refs[-2:]
    wide[...] = in_ref[...].reshape(4096, 128).astype(F32)
    for s in range(4):
        for t in range(8):
            for core in range(2):
                got = wide[pl.ds(core * 32 + t * 4 + s, 64, stride=64), :]
                out_ref[s, pl.ds(t * 128 + core * 64, 64), :] = got.astype(BF16)


def put_in_order(half, received, before):
    vmem = pl.BlockSpec(memory_space=pltpu.VMEM)
    args = [received] if before is None else [received, before]
    return pl.pallas_call(
        order_kernel,
        grid=(1,),
        in_specs=[vmem] + [pl.BlockSpec(memory_space=pl.ANY)] * (len(args) - 1),
        out_specs=pl.BlockSpec((4, 1024, 128), lambda g: (half, 0, 0)),
        out_shape=jax.ShapeDtypeStruct((8, 1024, 128), BF16),
        input_output_aliases={} if before is None else {1: 0},
        scratch_shapes=[pltpu.VMEM((4096, 128), F32)],
        compiler_params=pltpu.CompilerParams(vmem_limit_bytes=32 * 2**20),
    )(*args)


def index_of(xl, z, core, xh, y):
    return (((xl * 4 + z) * 2 + core) * 2 + xh) * 4 + y


def partners(orders, flips):
    pairs = []
    for xl in range(2):
        for z in range(4):
            for core in range(2):
                for xh in range(2):
                    for y in range(4):
                        place = {"x": xh * 2 + xl, "y": y, "z": z}
                        for axis, flip in zip(orders[core], flips):
                            place[axis] ^= flip
                        to = index_of(place["x"] % 2, place["z"], core, place["x"] // 2, place["y"])
                        pairs.append((index_of(xl, z, core, xh, y), to))
    return pairs


ORDERS = (("x", "y", "z"), ("y", "z", "x"))


def from_partners(held, flips):
    return lax.ppermute(held, ALL, partners(ORDERS, flips))


def from_line(held):
    return [from_partners(held, (0, 0, flip)) for flip in (1, 2, 3)]


def other_core(held):
    return lax.ppermute(held, "core", [(0, 1), (1, 0)])


def body(pair, chain_ids, block_mask, w_query, w_key, w_value, w_gate, w_bias, w_out):
    at = {name: lax.axis_index(name) for name in ALL}
    column = at["core"] * 64 + lax.axis_index(("xh", "y", "xl", "z"))
    mine = lax.dynamic_slice_in_dim(chain_ids.reshape(8, 128), column, 1, 1)
    lo = jnp.sum((chain_ids[None, :] < mine).astype(jnp.int32), axis=1)
    hi = jnp.sum((chain_ids[None, :] <= mine).astype(jnp.int32), axis=1)
    place = jnp.stack([at["xh"] * 2 + at["xl"], at["y"], at["z"], at["core"]] + [at["z"] * 0] * 4)
    info = jnp.stack([lo, hi, place]).astype(jnp.int32)
    bias = bias_of(pair, jnp.pad(w_bias.T, ((0, 12), (0, 0))))
    x = lax.all_to_all(pair, ("xh", "y", "xl", "z"), split_axis=0, concat_axis=0, tiled=True)
    held = jnp.concatenate([bias] + [from_partners(bias, (n, 0, 0)) for n in (1, 2, 3)], axis=1)
    held, x, info = lax.optimization_barrier((held, x, info))
    pieces = [held] + [from_partners(held, (0, n, 0)) for n in (1, 2, 3)]
    halves = [jnp.concatenate([p[n] for p in pieces], axis=0) for n in range(2)]
    x = norm_rows(x)
    halves[0], x = lax.optimization_barrier((halves[0], x))
    parts = [halves[0]] + from_line(halves[0])
    *parts, later = lax.optimization_barrier((*parts, halves[1]))
    first = parts + [other_core(p) for p in parts]
    second = [later] + from_line(later)
    x = x.reshape(8, 8, 2, 64, 128)
    weights = (w_query, w_key, w_value, w_gate, w_out)
    done = None
    backs = []
    for n in range(2):
        if n == 1:
            update, *second = lax.optimization_barrier((update, *second))
            backs.append(lax.all_to_all(update, ("xh", "y", "xl", "z", "core"), split_axis=0, concat_axis=0, tiled=True))
            second = second + [other_core(p) for p in second]
        update = attend(n, info, block_mask, x, weights, second if n else first)
    backs.append(lax.all_to_all(update, ("xh", "y", "xl", "z", "core"), split_axis=0, concat_axis=0, tiled=True))
    for n in range(2):
        done = put_in_order(n, backs[n], done)
    return done.reshape(1, 1, 8, 1024, 128)


def solution(mesh):
    fine = Mesh(mesh.devices.reshape(SIZES), ALL)
    row, col = ("xl", "z", "core"), ("xh", "y")
    return jax.shard_map(
        body,
        mesh=fine,
        in_specs=(P(row, col, None), P(), P(), P(), P(), P(), P(), P(), P()),
        out_specs=P(col, row, None, None, None),
        check_vma=False,
    )
```

```python
import math

import jax
import jax.numpy as jnp
from jax import lax
from jax.experimental import pallas as pl
from jax.experimental.pallas import tpu as pltpu
from jax.sharding import Mesh, PartitionSpec as P

ALL = ("xl", "z", "core", "xh", "y")
SIZES = (2, 4, 2, 2, 4)
LOG2E = math.log2(math.e)
SCALE = 32.0 ** -0.5
LEAST = 1e-25
MOST = 1e30
STEP = 1024
NT = (((1,), (1,)), ((), ()))
F32 = jnp.float32
BF16 = jnp.bfloat16


def dot(a, b):
    return jnp.dot(a, b, preferred_element_type=F32)


def dot_nt(a, b):
    return lax.dot_general(a, b, NT, preferred_element_type=F32)


def layer_normed(narrow):
    wide = narrow.astype(F32)
    center = jnp.mean(wide, axis=-1, keepdims=True)
    off = wide - center
    spread = jnp.mean(off * off, axis=-1, keepdims=True)
    return (off * lax.rsqrt(spread + 1e-5)).astype(BF16)


def bias_kernel(pair_ref, wb_ref, bias_ref):
    rows = [dot_nt(wb_ref[...], layer_normed(pair_ref[i])) for i in range(32)]
    for h in range(4):
        bias_ref[0, h] = jnp.concatenate([r[h : h + 1] for r in rows], axis=0).astype(BF16)


def bias_of(pair, wb):
    return pl.pallas_call(
        bias_kernel,
        grid=(2,),
        in_specs=[
            pl.BlockSpec((32, 128, 128), lambda g: (g, 0, 0)),
            pl.BlockSpec((16, 128), lambda g: (0, 0)),
        ],
        out_specs=pl.BlockSpec((1, 4, 32, 128), lambda g: (0, 0, g, 0)),
        out_shape=jax.ShapeDtypeStruct((1, 4, 64, 128), BF16),
    )(pair, wb)


def norm_kernel(x_ref, normed_ref):
    ones = jnp.ones((384, 128), BF16)
    for i in range(0, 16, 8):
        narrow = x_ref[i : i + 8].reshape(1024, 128)
        off = narrow.astype(F32) - dot(narrow, ones[:128]) * (1.0 / 128)
        left = off * off
        terms = []
        for _ in range(3):
            terms.append(left.astype(BF16))
            left = left - terms[-1].astype(F32)
        spread = dot(jnp.concatenate(terms, axis=1), ones) * (1.0 / 128)
        normed_ref[i : i + 8] = (off * lax.rsqrt(spread + 1e-5)).reshape(8, 128, 128).astype(BF16)


def norm_rows(x):
    block = pl.BlockSpec((16, 128, 128), lambda g: (g, 0, 0))
    return pl.pallas_call(
        norm_kernel,
        grid=(4,),
        in_specs=[block],
        out_specs=block,
        out_shape=jax.ShapeDtypeStruct((64, 128, 128), BF16),
        cost_estimate=pl.CostEstimate(flops=10**8, bytes_accessed=20 * 2**20, transcendentals=0),
    )(x)


def tile_in_use(info, mask, t, kt):
    return (mask[t, kt] == 1) | ((info[1, t] > kt * 128) & (info[0, t] < kt * 128 + 128))


def attend_kernel(info, mask, x_ref, wq, wk, wv, wg, wo, a0, a1, a2, a3, a4, a5, a6, a7,
                  out_ref, tiles, w_s, q_ref, k_ref, v_ref, gates, bias_s, kb0, kb1, vb0, vb1, p0, p1, acc, top, sems):
    copies = [
        pltpu.make_async_copy(ref, bias_s.at[pl.ds(n * 16, 16)], sems.at[n])
        for n, ref in enumerate((a0, a1, a2, a3, a4, a5, a6, a7))
    ]
    for copy in copies:
        copy.start()
    px, py, pz, core = info[2, 0], info[2, 1], info[2, 2], info[2, 3]
    here = (core * 64 + pz * 16 + py * 4 + px, (1 - core) * 64 + px * 16 + pz * 4 + py)
    lane = lax.broadcasted_iota(jnp.int32, (128, 128), 1) // 32
    spot = lax.broadcasted_iota(jnp.int32, (128, 128), 0)
    spot_lanes = lax.broadcasted_iota(jnp.int32, (64, 128), 1)

    def add(e, n):
        tiles[n] = e
        return n + tile_in_use(info, mask, e // 8, e % 8).astype(jnp.int32)

    count = lax.fori_loop(0, 64, add, 0)
    tiles[count] = -1
    tiles[count + 1] = -1

    w_s[0] = jnp.concatenate([wk[...], wv[...]], axis=1)
    w_s[1] = jnp.concatenate([wq[...], wg[...]], axis=1)

    def project(t, carry):
        both = dot(x_ref[:, t].reshape(1024, 128), w_s[0]).astype(BF16)
        k_ref[t] = both[:, :128]
        v_ref[t] = both[:, 128:]
        both = dot(x_ref[:, t].reshape(1024, 128), w_s[1])
        q_ref[t] = both[:, :128].astype(BF16)
        gates[t] = 1.0 / (1.0 + jnp.exp2(both[:, 128:] * -LOG2E))
        acc[t] = jnp.zeros((1024, 256), F32)
        return carry

    lax.fori_loop(0, 8, project, 0)

    def bounds(t, kt, valid):
        whole = (mask[t, kt] == 1) & valid
        lo = jnp.where(valid, jnp.where(whole, 0, info[0, t]), 5000)
        hi = jnp.where(valid, jnp.where(whole, 5000, info[1, t]), 0)
        return lo - kt * 128, hi - kt * 128

    def entry(n):
        e = tiles[n]
        held = jnp.maximum(e, 0)
        return held // 8, held % 8, e >= 0

    def block(ref, t, kt):
        return ref[t, pl.ds(pl.multiple_of(kt * 128, 128), 128), :]

    def pack_keys(t, kt, kb):
        keys = block(k_ref, t, kt)
        for h in range(4):
            kb[h * 128 : (h + 1) * 128, :] = jnp.where(lane == h, keys, jnp.zeros_like(keys))

    def pack_values(t, kt, valid, vb):
        lo, hi = bounds(t, kt, valid)
        allowed = (spot >= lo) & (spot < hi)
        values = block(v_ref, t, kt).astype(F32)
        for h in range(4):
            mine = (lane == h) & allowed
            vb[h * 128 : (h + 1) * 128, :128] = jnp.where(mine, values, 0.0).astype(BF16)
            vb[h * 128 : (h + 1) * 128, 128:] = jnp.where(mine, 1.0, 0.0).astype(BF16)

    def bias_tiles(g, kt):
        xl, z = g // 4, g % 4
        xh, y = kt // 4, kt % 4
        at0 = here[0] ^ (z * 16 + xl) ^ (y * 4 + xh * 2)
        at1 = here[1] ^ (xl * 16 + z * 4) ^ (xh * 32 + y)
        return at0, at1

    def scores(s, at, h):
        return (s * SCALE + bias_s[at, h].astype(F32)) * LOG2E

    def scored(t, kt, kb, use, first, count):
        s = dot_nt(q_ref[t, first : first + count, :], kb[...])
        for g in range(count // 128):
            for part, at in enumerate(bias_tiles(first // 128 + g, kt)):
                start = g * 128 + part * 64
                for h in range(4):
                    z = scores(s[start : start + 64, h * 128 : (h + 1) * 128], at, h)
                    use(slice(first + start, first + start + 64), h, z)

    def weigh(t, kt, kb, p, first, count):
        def seen(rows, h, z):
            p[rows, h * 128 : (h + 1) * 128] = jnp.exp2(z).astype(BF16)

        scored(t, kt, kb, seen, first, count)

    def mix(t, vb, p, first, count):
        rows = slice(first, first + count)
        acc[t, rows, :] += dot(p[rows, :], vb[...])

    p1[...] = jnp.zeros_like(p1)
    vb1[...] = jnp.zeros_like(vb1)
    t, kt, _ = entry(0)
    pack_keys(t, kt, kb0)
    for copy in copies:
        copy.wait()

    def two(m, carry):
        t0, kt0, valid0 = entry(2 * m)
        t1, kt1, valid1 = entry(2 * m + 1)
        t2, kt2, _ = entry(jnp.minimum(2 * m + 2, count))
        before, _, _ = entry(jnp.maximum(2 * m - 1, 0))
        for first in range(0, 1024, STEP):
            mix(before, vb1, p1, first, STEP)
            weigh(t0, kt0, kb0, p0, first, STEP)
        pack_values(t0, kt0, valid0, vb0)
        pack_keys(t1, kt1, kb1)
        for first in range(0, 1024, STEP):
            mix(t0, vb0, p0, first, STEP)
            weigh(t1, kt1, kb1, p1, first, STEP)
        pack_values(t1, kt1, valid1, vb1)
        pack_keys(t2, kt2, kb0)
        return carry

    pairs = (count + 1) // 2
    lax.fori_loop(0, pairs, two, 0)
    last, _, _ = entry(2 * pairs - 1)
    mix(last, vb1, p1, 0, 1024)

    def redo(t):
        top[...] = jnp.full_like(top, -3e38)
        acc[t] = jnp.zeros((1024, 256), F32)

        def per_tile(body):
            def step(kt, carry):
                @pl.when(tile_in_use(info, mask, t, kt))
                def _():
                    pack_keys(t, kt, kb0)
                    pack_values(t, kt, True, vb0)
                    body(kt)

                return carry

            lax.fori_loop(0, 8, step, 0)

        def find_top(kt):
            lo, hi = bounds(t, kt, True)
            allowed = (spot_lanes >= lo) & (spot_lanes < hi)

            def seen(rows, h, z):
                top[h, rows, :] = jnp.maximum(top[h, rows, :], jnp.where(allowed, z, -3e38))

            for first in range(0, 1024, STEP):
                scored(t, kt, kb0, seen, first, STEP)

        def add_up(kt):
            def seen(rows, h, z):
                p = jnp.exp2(jnp.minimum(z - top[h, rows, :], 0.0))
                p0[rows, h * 128 : (h + 1) * 128] = p.astype(BF16)

            for first in range(0, 1024, STEP):
                scored(t, kt, kb0, seen, first, STEP)
            mix(t, vb0, p0, 0, 1024)

        per_tile(find_top)
        for h in range(4):
            top[h] = jnp.broadcast_to(jnp.max(top[h], axis=-1, keepdims=True), (1024, 128))
        per_tile(add_up)

    def worst(t):
        total = acc[t, :, 128:]
        bad = jnp.where((total > LEAST) & (total < MOST), 0.0, 1.0)
        return jnp.max(bad.reshape(128, 8, 128), axis=0)

    def check(t, carry):
        @pl.when(jnp.max(worst(t)) > 0.5)
        def _():
            redo(t)

        return carry

    any_bad = lax.fori_loop(0, 8, lambda t, m: jnp.maximum(m, worst(t)), jnp.zeros((8, 128), F32))

    @pl.when(jnp.max(any_bad) > 0.5)
    def _():
        lax.fori_loop(0, 8, check, 0)

    for pair in range(4):
        updates = []
        for t in (2 * pair, 2 * pair + 1):
            a = acc[t]
            gated = (gates[t] * (a[:, :128] / a[:, 128:])).astype(BF16)
            updates.append(dot(gated, wo[...]).reshape(128, 8, 128))
        out_ref[:, pair * 16 : pair * 16 + 16, :] = jnp.concatenate(updates, axis=1).astype(BF16)


def attend(info, mask, x, weights, bias_parts):
    smem = pl.BlockSpec(memory_space=pltpu.SMEM)
    vmem = pl.BlockSpec(memory_space=pltpu.VMEM)
    hbm = pl.BlockSpec(memory_space=pl.ANY)
    return pl.pallas_call(
        attend_kernel,
        in_specs=[smem, smem] + [vmem] * 6 + [hbm] * 8,
        out_specs=vmem,
        out_shape=jax.ShapeDtypeStruct((128, 64, 128), BF16),
        scratch_shapes=[
            pltpu.SMEM((72,), jnp.int32),
            pltpu.VMEM((2, 128, 256), BF16),
            pltpu.VMEM((8, 1024, 128), BF16),
            pltpu.VMEM((8, 1024, 128), BF16),
            pltpu.VMEM((8, 1024, 128), BF16),
            pltpu.VMEM((8, 1024, 128), F32),
            pltpu.VMEM((128, 4, 64, 128), BF16),
            pltpu.VMEM((512, 128), BF16),
            pltpu.VMEM((512, 128), BF16),
            pltpu.VMEM((512, 256), BF16),
            pltpu.VMEM((512, 256), BF16),
            pltpu.VMEM((1024, 512), BF16),
            pltpu.VMEM((1024, 512), BF16),
            pltpu.VMEM((8, 1024, 256), F32),
            pltpu.VMEM((4, 1024, 128), F32),
            pltpu.SemaphoreType.DMA((8,)),
        ],
        compiler_params=pltpu.CompilerParams(vmem_limit_bytes=60 * 2**20),
        cost_estimate=pl.CostEstimate(flops=20 * 10**9, bytes_accessed=12 * 2**20, transcendentals=11 * 10**6),
    )(info, mask, x, *weights, *bias_parts)


def order_kernel(in_ref, out_ref, wide):
    wide[...] = in_ref[...].reshape(2048, 128).astype(F32)
    for s in range(8):
        for t in range(2):
            for core in range(2):
                got = wide[pl.ds(core * 16 + t * 8 + s, 64, stride=32), :]
                out_ref[s, pl.ds(t * 128 + core * 64, 64), :] = got.astype(BF16)


def put_in_order(received):
    return pl.pallas_call(
        order_kernel,
        grid=(4,),
        in_specs=[pl.BlockSpec((128, 16, 128), lambda g: (0, g, 0))],
        out_specs=pl.BlockSpec((8, 256, 128), lambda g: (0, g, 0)),
        out_shape=jax.ShapeDtypeStruct((8, 1024, 128), BF16),
        scratch_shapes=[pltpu.VMEM((2048, 128), F32)],
        compiler_params=pltpu.CompilerParams(vmem_limit_bytes=32 * 2**20),
    )(received)


def index_of(xl, z, core, xh, y):
    return (((xl * 4 + z) * 2 + core) * 2 + xh) * 4 + y


def partners(orders, flips):
    pairs = []
    for xl in range(2):
        for z in range(4):
            for core in range(2):
                for xh in range(2):
                    for y in range(4):
                        place = {"x": xh * 2 + xl, "y": y, "z": z}
                        for axis, flip in zip(orders[core], flips):
                            place[axis] ^= flip
                        to = index_of(place["x"] % 2, place["z"], core, place["x"] // 2, place["y"])
                        pairs.append((index_of(xl, z, core, xh, y), to))
    return pairs


ORDERS = (("x", "y", "z"), ("y", "z", "x"))


def from_partners(held, flips):
    return lax.ppermute(held, ALL, partners(ORDERS, flips))


def from_line(held):
    return [from_partners(held, (0, 0, flip)) for flip in (1, 2, 3)]


def other_core(held):
    return lax.ppermute(held, "core", [(0, 1), (1, 0)])


def body(pair, chain_ids, block_mask, w_query, w_key, w_value, w_gate, w_bias, w_out):
    at = {name: lax.axis_index(name) for name in ALL}
    column = at["core"] * 64 + lax.axis_index(("xh", "y", "xl", "z"))
    mine = lax.dynamic_slice_in_dim(chain_ids.reshape(8, 128), column, 1, 1)
    lo = jnp.sum((chain_ids[None, :] < mine).astype(jnp.int32), axis=1)
    hi = jnp.sum((chain_ids[None, :] <= mine).astype(jnp.int32), axis=1)
    place = jnp.stack([at["xh"] * 2 + at["xl"], at["y"], at["z"], at["core"]] + [at["z"] * 0] * 4)
    info = jnp.stack([lo, hi, place]).astype(jnp.int32)
    bias = bias_of(pair, jnp.pad(w_bias.T, ((0, 12), (0, 0))))
    x = lax.all_to_all(pair, ("xh", "y", "xl", "z"), split_axis=0, concat_axis=0, tiled=True)
    held = jnp.concatenate([bias] + [from_partners(bias, (n, 0, 0)) for n in (1, 2, 3)], axis=0)
    held, x, info = lax.optimization_barrier((held, x, info))
    held = jnp.concatenate([held] + [from_partners(held, (0, n, 0)) for n in (1, 2, 3)], axis=0)
    x = norm_rows(x)
    held, x = lax.optimization_barrier((held, x))
    parts = [held] + from_line(held)
    parts = parts + [other_core(p) for p in parts]
    weights = (w_query, w_key, w_value, w_gate, w_out)
    update = attend(info, block_mask, x.reshape(8, 8, 128, 128), weights, parts)
    back = lax.all_to_all(update, ("xh", "y", "xl", "z", "core"), split_axis=0, concat_axis=0, tiled=True)
    return put_in_order(back).reshape(1, 1, 8, 1024, 128)


def solution(mesh):
    fine = Mesh(mesh.devices.reshape(SIZES), ALL)
    row, col = ("xl", "z", "core"), ("xh", "y")
    return jax.shard_map(
        body,
        mesh=fine,
        in_specs=(P(row, col, None), P(), P(), P(), P(), P(), P(), P(), P()),
        out_specs=P(col, row, None, None, None),
        check_vma=False,
    )
```

```python
import math

import jax
import jax.numpy as jnp
from jax import lax
from jax.experimental import pallas as pl
from jax.experimental.pallas import tpu as pltpu
from jax.sharding import Mesh, PartitionSpec as P

ALL = ("xl", "z", "core", "xh", "y")
SIZES = (2, 4, 2, 2, 4)
LOG2E = math.log2(math.e)
SCALE = 32.0 ** -0.5
LEAST = 1e-25
MOST = 1e30
STEP = 1024
NT = (((1,), (1,)), ((), ()))
F32 = jnp.float32
BF16 = jnp.bfloat16


def dot(a, b):
    return jnp.dot(a, b, preferred_element_type=F32)


def dot_nt(a, b):
    return lax.dot_general(a, b, NT, preferred_element_type=F32)


def layer_normed(narrow):
    ones = jnp.ones((384, 128), BF16)
    off = narrow.astype(F32) - dot(narrow, ones[:128]) * (1.0 / 128)
    left = off * off
    terms = []
    for _ in range(3):
        terms.append(left.astype(BF16))
        left = left - terms[-1].astype(F32)
    spread = dot(jnp.concatenate(terms, axis=1), ones) * (1.0 / 128)
    return (off * lax.rsqrt(spread + 1e-5)).astype(BF16)


def norm_kernel(pair_ref, wb_ref, normed_ref, bias_ref):
    rows = []
    for i in range(0, 32, 16):
        normed = layer_normed(pair_ref[i : i + 16].reshape(2048, 128))
        normed_ref[i : i + 16] = normed.reshape(16, 128, 128)
        biases = dot_nt(wb_ref[...], normed)
        rows += [biases[:, n * 128 : (n + 1) * 128] for n in range(16)]
    for h in range(4):
        bias_ref[0, h] = jnp.concatenate([r[h : h + 1] for r in rows], axis=0).astype(BF16)


def norm_and_bias(pair, wb):
    return pl.pallas_call(
        norm_kernel,
        grid=(2,),
        in_specs=[
            pl.BlockSpec((32, 128, 128), lambda g: (g, 0, 0)),
            pl.BlockSpec((4, 128), lambda g: (0, 0)),
        ],
        out_specs=[
            pl.BlockSpec((32, 128, 128), lambda g: (g, 0, 0)),
            pl.BlockSpec((1, 4, 32, 128), lambda g: (0, 0, g, 0)),
        ],
        out_shape=[
            jax.ShapeDtypeStruct((64, 128, 128), BF16),
            jax.ShapeDtypeStruct((1, 4, 64, 128), BF16),
        ],
    )(pair, wb)


def tile_in_use(info, mask, t, kt):
    return (mask[t, kt] == 1) | ((info[1, t] > kt * 128) & (info[0, t] < kt * 128 + 128))


def attend_kernel(info, mask, x_ref, wq, wk, wv, wg, wo, a0, a1, a2, a3, a4, a5, a6, a7,
                  out_ref, tiles, w_s, q_ref, k_ref, v_ref, gates, bias_s, kb0, kb1, vb0, vb1, p0, p1, acc, top, sems):
    copies = [
        pltpu.make_async_copy(ref, bias_s.at[pl.ds(n * 16, 16)], sems.at[n])
        for n, ref in enumerate((a0, a1, a2, a3, a4, a5, a6, a7))
    ]
    for copy in copies:
        copy.start()
    px, py, pz, core = info[2, 0], info[2, 1], info[2, 2], info[2, 3]
    here = (core * 64 + pz * 16 + py * 4 + px, (1 - core) * 64 + px * 16 + pz * 4 + py)
    lane = lax.broadcasted_iota(jnp.int32, (128, 128), 1) // 32
    spot = lax.broadcasted_iota(jnp.int32, (128, 128), 0)
    spot_lanes = lax.broadcasted_iota(jnp.int32, (64, 128), 1)

    def add(e, n):
        tiles[n] = e
        return n + tile_in_use(info, mask, e // 8, e % 8).astype(jnp.int32)

    count = lax.fori_loop(0, 64, add, 0)
    tiles[count] = -1
    tiles[count + 1] = -1

    w_s[0] = jnp.concatenate([wk[...], wv[...]], axis=1)
    w_s[1] = jnp.concatenate([wq[...], wg[...]], axis=1)

    def project(t, carry):
        both = dot(x_ref[:, t].reshape(1024, 128), w_s[0]).astype(BF16)
        k_ref[t] = both[:, :128]
        v_ref[t] = both[:, 128:]
        both = dot(x_ref[:, t].reshape(1024, 128), w_s[1])
        q_ref[t] = both[:, :128].astype(BF16)
        gates[t] = 1.0 / (1.0 + jnp.exp2(both[:, 128:] * -LOG2E))
        acc[t] = jnp.zeros((1024, 256), F32)
        return carry

    lax.fori_loop(0, 8, project, 0)

    def bounds(t, kt, valid):
        whole = (mask[t, kt] == 1) & valid
        lo = jnp.where(valid, jnp.where(whole, 0, info[0, t]), 5000)
        hi = jnp.where(valid, jnp.where(whole, 5000, info[1, t]), 0)
        return lo - kt * 128, hi - kt * 128

    def entry(n):
        e = tiles[n]
        held = jnp.maximum(e, 0)
        return held // 8, held % 8, e >= 0

    def block(ref, t, kt):
        return ref[t, pl.ds(pl.multiple_of(kt * 128, 128), 128), :]

    def pack_keys(t, kt, kb):
        keys = block(k_ref, t, kt)
        for h in range(4):
            kb[h * 128 : (h + 1) * 128, :] = jnp.where(lane == h, keys, jnp.zeros_like(keys))

    def pack_values(t, kt, valid, vb):
        lo, hi = bounds(t, kt, valid)
        allowed = (spot >= lo) & (spot < hi)
        values = block(v_ref, t, kt).astype(F32)
        for h in range(4):
            mine = (lane == h) & allowed
            vb[h * 128 : (h + 1) * 128, :128] = jnp.where(mine, values, 0.0).astype(BF16)
            vb[h * 128 : (h + 1) * 128, 128:] = jnp.where(mine, 1.0, 0.0).astype(BF16)

    def bias_tiles(g, kt):
        xl, z = g // 4, g % 4
        xh, y = kt // 4, kt % 4
        at0 = here[0] ^ (z * 16 + xl) ^ (y * 4 + xh * 2)
        at1 = here[1] ^ (xl * 16 + z * 4) ^ (xh * 32 + y)
        return at0, at1

    def scores(s, at, h):
        return (s * SCALE + bias_s[at, h].astype(F32)) * LOG2E

    def scored(t, kt, kb, use, first, count):
        s = dot_nt(q_ref[t, first : first + count, :], kb[...])
        for g in range(count // 128):
            for part, at in enumerate(bias_tiles(first // 128 + g, kt)):
                start = g * 128 + part * 64
                for h in range(4):
                    z = scores(s[start : start + 64, h * 128 : (h + 1) * 128], at, h)
                    use(slice(first + start, first + start + 64), h, z)

    def weigh(t, kt, kb, p, first, count):
        def seen(rows, h, z):
            p[rows, h * 128 : (h + 1) * 128] = jnp.exp2(z).astype(BF16)

        scored(t, kt, kb, seen, first, count)

    def mix(t, vb, p, first, count):
        rows = slice(first, first + count)
        acc[t, rows, :] += dot(p[rows, :], vb[...])

    p1[...] = jnp.zeros_like(p1)
    vb1[...] = jnp.zeros_like(vb1)
    t, kt, _ = entry(0)
    pack_keys(t, kt, kb0)
    for copy in copies:
        copy.wait()

    def two(m, carry):
        t0, kt0, valid0 = entry(2 * m)
        t1, kt1, valid1 = entry(2 * m + 1)
        t2, kt2, _ = entry(jnp.minimum(2 * m + 2, count))
        before, _, _ = entry(jnp.maximum(2 * m - 1, 0))
        for first in range(0, 1024, STEP):
            mix(before, vb1, p1, first, STEP)
            weigh(t0, kt0, kb0, p0, first, STEP)
        pack_values(t0, kt0, valid0, vb0)
        pack_keys(t1, kt1, kb1)
        for first in range(0, 1024, STEP):
            mix(t0, vb0, p0, first, STEP)
            weigh(t1, kt1, kb1, p1, first, STEP)
        pack_values(t1, kt1, valid1, vb1)
        pack_keys(t2, kt2, kb0)
        return carry

    pairs = (count + 1) // 2
    lax.fori_loop(0, pairs, two, 0)
    last, _, _ = entry(2 * pairs - 1)
    mix(last, vb1, p1, 0, 1024)

    def redo(t):
        top[...] = jnp.full_like(top, -3e38)
        acc[t] = jnp.zeros((1024, 256), F32)

        def per_tile(body):
            def step(kt, carry):
                @pl.when(tile_in_use(info, mask, t, kt))
                def _():
                    pack_keys(t, kt, kb0)
                    pack_values(t, kt, True, vb0)
                    body(kt)

                return carry

            lax.fori_loop(0, 8, step, 0)

        def find_top(kt):
            lo, hi = bounds(t, kt, True)
            allowed = (spot_lanes >= lo) & (spot_lanes < hi)

            def seen(rows, h, z):
                top[h, rows, :] = jnp.maximum(top[h, rows, :], jnp.where(allowed, z, -3e38))

            for first in range(0, 1024, STEP):
                scored(t, kt, kb0, seen, first, STEP)

        def add_up(kt):
            def seen(rows, h, z):
                p = jnp.exp2(jnp.minimum(z - top[h, rows, :], 0.0))
                p0[rows, h * 128 : (h + 1) * 128] = p.astype(BF16)

            for first in range(0, 1024, STEP):
                scored(t, kt, kb0, seen, first, STEP)
            mix(t, vb0, p0, 0, 1024)

        per_tile(find_top)
        for h in range(4):
            top[h] = jnp.broadcast_to(jnp.max(top[h], axis=-1, keepdims=True), (1024, 128))
        per_tile(add_up)

    def worst(t):
        total = acc[t, :, 128:]
        bad = jnp.where((total > LEAST) & (total < MOST), 0.0, 1.0)
        return jnp.max(bad.reshape(128, 8, 128), axis=0)

    def check(t, carry):
        @pl.when(jnp.max(worst(t)) > 0.5)
        def _():
            redo(t)

        return carry

    any_bad = lax.fori_loop(0, 8, lambda t, m: jnp.maximum(m, worst(t)), jnp.zeros((8, 128), F32))

    @pl.when(jnp.max(any_bad) > 0.5)
    def _():
        lax.fori_loop(0, 8, check, 0)

    for pair in range(4):
        updates = []
        for t in (2 * pair, 2 * pair + 1):
            a = acc[t]
            gated = (gates[t] * (a[:, :128] / a[:, 128:])).astype(BF16)
            updates.append(dot(gated, wo[...]).reshape(128, 8, 128))
        out_ref[:, pair * 16 : pair * 16 + 16, :] = jnp.concatenate(updates, axis=1).astype(BF16)


def attend(info, mask, x, weights, bias_parts):
    smem = pl.BlockSpec(memory_space=pltpu.SMEM)
    vmem = pl.BlockSpec(memory_space=pltpu.VMEM)
    hbm = pl.BlockSpec(memory_space=pl.ANY)
    return pl.pallas_call(
        attend_kernel,
        in_specs=[smem, smem] + [vmem] * 6 + [hbm] * 8,
        out_specs=vmem,
        out_shape=jax.ShapeDtypeStruct((128, 64, 128), BF16),
        scratch_shapes=[
            pltpu.SMEM((72,), jnp.int32),
            pltpu.VMEM((2, 128, 256), BF16),
            pltpu.VMEM((8, 1024, 128), BF16),
            pltpu.VMEM((8, 1024, 128), BF16),
            pltpu.VMEM((8, 1024, 128), BF16),
            pltpu.VMEM((8, 1024, 128), F32),
            pltpu.VMEM((128, 4, 64, 128), BF16),
            pltpu.VMEM((512, 128), BF16),
            pltpu.VMEM((512, 128), BF16),
            pltpu.VMEM((512, 256), BF16),
            pltpu.VMEM((512, 256), BF16),
            pltpu.VMEM((1024, 512), BF16),
            pltpu.VMEM((1024, 512), BF16),
            pltpu.VMEM((8, 1024, 256), F32),
            pltpu.VMEM((4, 1024, 128), F32),
            pltpu.SemaphoreType.DMA((8,)),
        ],
        compiler_params=pltpu.CompilerParams(vmem_limit_bytes=60 * 2**20),
        cost_estimate=pl.CostEstimate(flops=20 * 10**9, bytes_accessed=12 * 2**20, transcendentals=11 * 10**6),
    )(info, mask, x, *weights, *bias_parts)


def order_kernel(in_ref, out_ref, wide):
    wide[...] = in_ref[...].reshape(2048, 128).astype(F32)
    for s in range(8):
        for t in range(2):
            for core in range(2):
                got = wide[pl.ds(core * 16 + t * 8 + s, 64, stride=32), :]
                out_ref[s, pl.ds(t * 128 + core * 64, 64), :] = got.astype(BF16)


def put_in_order(received):
    return pl.pallas_call(
        order_kernel,
        grid=(4,),
        in_specs=[pl.BlockSpec((128, 16, 128), lambda g: (0, g, 0))],
        out_specs=pl.BlockSpec((8, 256, 128), lambda g: (0, g, 0)),
        out_shape=jax.ShapeDtypeStruct((8, 1024, 128), BF16),
        scratch_shapes=[pltpu.VMEM((2048, 128), F32)],
        compiler_params=pltpu.CompilerParams(vmem_limit_bytes=32 * 2**20),
    )(received)


def index_of(xl, z, core, xh, y):
    return (((xl * 4 + z) * 2 + core) * 2 + xh) * 4 + y


def partners(orders, flips):
    pairs = []
    for xl in range(2):
        for z in range(4):
            for core in range(2):
                for xh in range(2):
                    for y in range(4):
                        place = {"x": xh * 2 + xl, "y": y, "z": z}
                        for axis, flip in zip(orders[core], flips):
                            place[axis] ^= flip
                        to = index_of(place["x"] % 2, place["z"], core, place["x"] // 2, place["y"])
                        pairs.append((index_of(xl, z, core, xh, y), to))
    return pairs


ORDERS = (("x", "y", "z"), ("y", "z", "x"))


def from_partners(held, flips):
    return lax.ppermute(held, ALL, partners(ORDERS, flips))


def from_line(held):
    return [from_partners(held, (0, 0, flip)) for flip in (1, 2, 3)]


def other_core(held):
    return lax.ppermute(held, "core", [(0, 1), (1, 0)])


def body(pair, chain_ids, block_mask, w_query, w_key, w_value, w_gate, w_bias, w_out):
    at = {name: lax.axis_index(name) for name in ALL}
    column = at["core"] * 64 + lax.axis_index(("xh", "y", "xl", "z"))
    mine = lax.dynamic_slice_in_dim(chain_ids.reshape(8, 128), column, 1, 1)
    lo = jnp.sum((chain_ids[None, :] < mine).astype(jnp.int32), axis=1)
    hi = jnp.sum((chain_ids[None, :] <= mine).astype(jnp.int32), axis=1)
    place = jnp.stack([at["xh"] * 2 + at["xl"], at["y"], at["z"], at["core"]] + [at["z"] * 0] * 4)
    info = jnp.stack([lo, hi, place]).astype(jnp.int32)
    normed, bias = norm_and_bias(pair, w_bias.T)
    held = jnp.concatenate([bias] + [from_partners(bias, (n, 0, 0)) for n in (1, 2, 3)], axis=0)
    held, info = lax.optimization_barrier((held, info))
    held = jnp.concatenate([held] + [from_partners(held, (0, n, 0)) for n in (1, 2, 3)], axis=0)
    held, normed = lax.optimization_barrier((held, normed))
    parts = [held] + from_line(held)
    parts = parts + [other_core(p) for p in parts]
    x = lax.all_to_all(normed, ("xh", "y", "xl", "z"), split_axis=0, concat_axis=0, tiled=True)
    weights = (w_query, w_key, w_value, w_gate, w_out)
    update = attend(info, block_mask, x.reshape(8, 8, 128, 128), weights, parts)
    back = lax.all_to_all(update, ("xh", "y", "xl", "z", "core"), split_axis=0, concat_axis=0, tiled=True)
    return put_in_order(back).reshape(1, 1, 8, 1024, 128)


def solution(mesh):
    fine = Mesh(mesh.devices.reshape(SIZES), ALL)
    row, col = ("xl", "z", "core"), ("xh", "y")
    return jax.shard_map(
        body,
        mesh=fine,
        in_specs=(P(row, col, None), P(), P(), P(), P(), P(), P(), P(), P()),
        out_specs=P(col, row, None, None, None),
        check_vma=False,
    )
```

```python
import math

import jax
import jax.numpy as jnp
from jax import lax
from jax.experimental import pallas as pl
from jax.experimental.pallas import tpu as pltpu
from jax.sharding import Mesh, PartitionSpec as P

ALL = ("xl", "z", "core", "xh", "y")
SIZES = (2, 4, 2, 2, 4)
LOG2E = math.log2(math.e)
SCALE = 32.0 ** -0.5
LEAST = 1e-25
MOST = 1e30
STEP = 1024
NT = (((1,), (1,)), ((), ()))
F32 = jnp.float32
BF16 = jnp.bfloat16


def dot(a, b):
    return jnp.dot(a, b, preferred_element_type=F32)


def dot_nt(a, b):
    return lax.dot_general(a, b, NT, preferred_element_type=F32)


def layer_normed(narrow):
    ones = jnp.ones((384, 128), BF16)
    off = narrow.astype(F32) - dot(narrow, ones[:128]) * (1.0 / 128)
    left = off * off
    terms = []
    for _ in range(3):
        terms.append(left.astype(BF16))
        left = left - terms[-1].astype(F32)
    spread = dot(jnp.concatenate(terms, axis=1), ones) * (1.0 / 128)
    return (off * lax.rsqrt(spread + 1e-5)).astype(BF16)


def norm_kernel(pair_ref, wb_ref, normed_ref, bias_ref):
    rows = []
    for i in range(0, 32, 16):
        normed = layer_normed(pair_ref[i : i + 16].reshape(2048, 128))
        normed_ref[i : i + 16] = normed.reshape(16, 128, 128)
        biases = dot_nt(wb_ref[...], normed)
        rows += [biases[:, n * 128 : (n + 1) * 128] for n in range(16)]
    for h in range(4):
        bias_ref[0, h] = jnp.concatenate([r[h : h + 1] for r in rows], axis=0).astype(BF16)


def norm_and_bias(pair, wb):
    return pl.pallas_call(
        norm_kernel,
        grid=(2,),
        in_specs=[
            pl.BlockSpec((32, 128, 128), lambda g: (g, 0, 0)),
            pl.BlockSpec((4, 128), lambda g: (0, 0)),
        ],
        out_specs=[
            pl.BlockSpec((32, 128, 128), lambda g: (g, 0, 0)),
            pl.BlockSpec((1, 4, 32, 128), lambda g: (0, 0, g, 0)),
        ],
        out_shape=[
            jax.ShapeDtypeStruct((64, 128, 128), BF16),
            jax.ShapeDtypeStruct((1, 4, 64, 128), BF16),
        ],
    )(pair, wb)


def tile_in_use(info, mask, t, kt):
    return (mask[t, kt] == 1) | ((info[1, t] > kt * 128) & (info[0, t] < kt * 128 + 128))


def attend_kernel(info, mask, x_hbm, wq, wk, wv, wg, wo, a0, a1, a2, a3, a4, a5, a6, a7,
                  out_hbm, x_ref, out_ref, tiles, w_s, q_ref, k_ref, v_ref, gates, bias_s, kb0, kb1, vb0, vb1, p0, p1, acc, top, sems, x_sems, out_sems):
    copies = [
        pltpu.make_async_copy(ref, bias_s.at[pl.ds(n * 16, 16)], sems.at[n])
        for n, ref in enumerate((a0, a1, a2, a3, a4, a5, a6, a7))
    ]
    def rows_of(t):
        return pltpu.make_async_copy(x_hbm.at[:, t], x_ref.at[:, t], x_sems.at[t])

    for t in range(8):
        rows_of(t).start()
    for copy in copies:
        copy.start()
    px, py, pz, core = info[2, 0], info[2, 1], info[2, 2], info[2, 3]
    here = (core * 64 + pz * 16 + py * 4 + px, (1 - core) * 64 + px * 16 + pz * 4 + py)
    lane = lax.broadcasted_iota(jnp.int32, (128, 128), 1) // 32
    spot = lax.broadcasted_iota(jnp.int32, (128, 128), 0)
    spot_lanes = lax.broadcasted_iota(jnp.int32, (64, 128), 1)

    def add(e, n):
        tiles[n] = e
        return n + tile_in_use(info, mask, e // 8, e % 8).astype(jnp.int32)

    count = lax.fori_loop(0, 64, add, 0)
    tiles[count] = -1
    tiles[count + 1] = -1

    w_s[0] = jnp.concatenate([wk[...], wv[...]], axis=1)
    w_s[1] = jnp.concatenate([wq[...], wg[...]], axis=1)

    def project(t, carry):
        rows_of(t).wait()
        both = dot(x_ref[:, t].reshape(1024, 128), w_s[0]).astype(BF16)
        k_ref[t] = both[:, :128]
        v_ref[t] = both[:, 128:]
        both = dot(x_ref[:, t].reshape(1024, 128), w_s[1])
        q_ref[t] = both[:, :128].astype(BF16)
        gates[t] = 1.0 / (1.0 + jnp.exp2(both[:, 128:] * -LOG2E))
        acc[t] = jnp.zeros((1024, 256), F32)
        return carry

    lax.fori_loop(0, 8, project, 0)

    def bounds(t, kt, valid):
        whole = (mask[t, kt] == 1) & valid
        lo = jnp.where(valid, jnp.where(whole, 0, info[0, t]), 5000)
        hi = jnp.where(valid, jnp.where(whole, 5000, info[1, t]), 0)
        return lo - kt * 128, hi - kt * 128

    def entry(n):
        e = tiles[n]
        held = jnp.maximum(e, 0)
        return held // 8, held % 8, e >= 0

    def block(ref, t, kt):
        return ref[t, pl.ds(pl.multiple_of(kt * 128, 128), 128), :]

    def pack_keys(t, kt, kb):
        keys = block(k_ref, t, kt)
        for h in range(4):
            kb[h * 128 : (h + 1) * 128, :] = jnp.where(lane == h, keys, jnp.zeros_like(keys))

    def pack_values(t, kt, valid, vb):
        lo, hi = bounds(t, kt, valid)
        allowed = (spot >= lo) & (spot < hi)
        values = block(v_ref, t, kt).astype(F32)
        for h in range(4):
            mine = (lane == h) & allowed
            vb[h * 128 : (h + 1) * 128, :128] = jnp.where(mine, values, 0.0).astype(BF16)
            vb[h * 128 : (h + 1) * 128, 128:] = jnp.where(mine, 1.0, 0.0).astype(BF16)

    def bias_tiles(g, kt):
        xl, z = g // 4, g % 4
        xh, y = kt // 4, kt % 4
        at0 = here[0] ^ (z * 16 + xl) ^ (y * 4 + xh * 2)
        at1 = here[1] ^ (xl * 16 + z * 4) ^ (xh * 32 + y)
        return at0, at1

    def scores(s, at, h):
        return (s * SCALE + bias_s[at, h].astype(F32)) * LOG2E

    def scored(t, kt, kb, use, first, count):
        s = dot_nt(q_ref[t, first : first + count, :], kb[...])
        for g in range(count // 128):
            for part, at in enumerate(bias_tiles(first // 128 + g, kt)):
                start = g * 128 + part * 64
                for h in range(4):
                    z = scores(s[start : start + 64, h * 128 : (h + 1) * 128], at, h)
                    use(slice(first + start, first + start + 64), h, z)

    def weigh(t, kt, kb, p, first, count):
        def seen(rows, h, z):
            p[rows, h * 128 : (h + 1) * 128] = jnp.exp2(z).astype(BF16)

        scored(t, kt, kb, seen, first, count)

    def mix(t, vb, p, first, count):
        rows = slice(first, first + count)
        acc[t, rows, :] += dot(p[rows, :], vb[...])

    p1[...] = jnp.zeros_like(p1)
    vb1[...] = jnp.zeros_like(vb1)
    t, kt, _ = entry(0)
    pack_keys(t, kt, kb0)
    for copy in copies:
        copy.wait()

    def two(m, carry):
        t0, kt0, valid0 = entry(2 * m)
        t1, kt1, valid1 = entry(2 * m + 1)
        t2, kt2, _ = entry(jnp.minimum(2 * m + 2, count))
        before, _, _ = entry(jnp.maximum(2 * m - 1, 0))
        for first in range(0, 1024, STEP):
            mix(before, vb1, p1, first, STEP)
            weigh(t0, kt0, kb0, p0, first, STEP)
        pack_values(t0, kt0, valid0, vb0)
        pack_keys(t1, kt1, kb1)
        for first in range(0, 1024, STEP):
            mix(t0, vb0, p0, first, STEP)
            weigh(t1, kt1, kb1, p1, first, STEP)
        pack_values(t1, kt1, valid1, vb1)
        pack_keys(t2, kt2, kb0)
        return carry

    pairs = (count + 1) // 2
    lax.fori_loop(0, pairs, two, 0)
    last, _, _ = entry(2 * pairs - 1)
    mix(last, vb1, p1, 0, 1024)

    def redo(t):
        top[...] = jnp.full_like(top, -3e38)
        acc[t] = jnp.zeros((1024, 256), F32)

        def per_tile(body):
            def step(kt, carry):
                @pl.when(tile_in_use(info, mask, t, kt))
                def _():
                    pack_keys(t, kt, kb0)
                    pack_values(t, kt, True, vb0)
                    body(kt)

                return carry

            lax.fori_loop(0, 8, step, 0)

        def find_top(kt):
            lo, hi = bounds(t, kt, True)
            allowed = (spot_lanes >= lo) & (spot_lanes < hi)

            def seen(rows, h, z):
                top[h, rows, :] = jnp.maximum(top[h, rows, :], jnp.where(allowed, z, -3e38))

            for first in range(0, 1024, STEP):
                scored(t, kt, kb0, seen, first, STEP)

        def add_up(kt):
            def seen(rows, h, z):
                p = jnp.exp2(jnp.minimum(z - top[h, rows, :], 0.0))
                p0[rows, h * 128 : (h + 1) * 128] = p.astype(BF16)

            for first in range(0, 1024, STEP):
                scored(t, kt, kb0, seen, first, STEP)
            mix(t, vb0, p0, 0, 1024)

        per_tile(find_top)
        for h in range(4):
            top[h] = jnp.broadcast_to(jnp.max(top[h], axis=-1, keepdims=True), (1024, 128))
        per_tile(add_up)

    def worst(t):
        total = acc[t, :, 128:]
        bad = jnp.where((total > LEAST) & (total < MOST), 0.0, 1.0)
        return jnp.max(bad.reshape(128, 8, 128), axis=0)

    def check(t, carry):
        @pl.when(jnp.max(worst(t)) > 0.5)
        def _():
            redo(t)

        return carry

    any_bad = lax.fori_loop(0, 8, lambda t, m: jnp.maximum(m, worst(t)), jnp.zeros((8, 128), F32))

    @pl.when(jnp.max(any_bad) > 0.5)
    def _():
        lax.fori_loop(0, 8, check, 0)

    def part_out(pair):
        return pltpu.make_async_copy(out_ref.at[pair], out_hbm.at[:, pair], out_sems.at[pair])

    for pair in range(4):
        updates = []
        for t in (2 * pair, 2 * pair + 1):
            a = acc[t]
            gated = (gates[t] * (a[:, :128] / a[:, 128:])).astype(BF16)
            updates.append(dot(gated, wo[...]).reshape(128, 8, 128))
        out_ref[pair] = jnp.concatenate(updates, axis=1).astype(BF16)
        part_out(pair).start()
    for pair in range(4):
        part_out(pair).wait()


def attend(info, mask, x, weights, bias_parts):
    smem = pl.BlockSpec(memory_space=pltpu.SMEM)
    vmem = pl.BlockSpec(memory_space=pltpu.VMEM)
    hbm = pl.BlockSpec(memory_space=pl.ANY)
    return pl.pallas_call(
        attend_kernel,
        in_specs=[smem, smem, hbm] + [vmem] * 5 + [hbm] * 8,
        out_specs=hbm,
        out_shape=jax.ShapeDtypeStruct((128, 4, 16, 128), BF16),
        scratch_shapes=[
            pltpu.VMEM((8, 8, 128, 128), BF16),
            pltpu.VMEM((4, 128, 16, 128), BF16),
            pltpu.SMEM((72,), jnp.int32),
            pltpu.VMEM((2, 128, 256), BF16),
            pltpu.VMEM((8, 1024, 128), BF16),
            pltpu.VMEM((8, 1024, 128), BF16),
            pltpu.VMEM((8, 1024, 128), BF16),
            pltpu.VMEM((8, 1024, 128), F32),
            pltpu.VMEM((128, 4, 64, 128), BF16),
            pltpu.VMEM((512, 128), BF16),
            pltpu.VMEM((512, 128), BF16),
            pltpu.VMEM((512, 256), BF16),
            pltpu.VMEM((512, 256), BF16),
            pltpu.VMEM((1024, 512), BF16),
            pltpu.VMEM((1024, 512), BF16),
            pltpu.VMEM((8, 1024, 256), F32),
            pltpu.VMEM((4, 1024, 128), F32),
            pltpu.SemaphoreType.DMA((8,)),
            pltpu.SemaphoreType.DMA((8,)),
            pltpu.SemaphoreType.DMA((4,)),
        ],
        compiler_params=pltpu.CompilerParams(vmem_limit_bytes=60 * 2**20),
        cost_estimate=pl.CostEstimate(flops=20 * 10**9, bytes_accessed=12 * 2**20, transcendentals=11 * 10**6),
    )(info, mask, x, *weights, *bias_parts)


def order_kernel(in_ref, out_ref):
    for t in range(2):
        held = in_ref[:, t * 8 : t * 8 + 8, :].astype(F32).reshape(64, 2, 8, 128)
        for core in range(2):
            turned = jnp.swapaxes(held[:, core], 0, 1)
            out_ref[:, t * 128 + core * 64 : t * 128 + core * 64 + 64, :] = turned.astype(BF16)


def put_in_order(received):
    return pl.pallas_call(
        order_kernel,
        grid=(4,),
        in_specs=[pl.BlockSpec((128, 16, 128), lambda g: (0, g, 0))],
        out_specs=pl.BlockSpec((8, 256, 128), lambda g: (0, g, 0)),
        out_shape=jax.ShapeDtypeStruct((8, 1024, 128), BF16),
        compiler_params=pltpu.CompilerParams(vmem_limit_bytes=32 * 2**20),
    )(received)


def index_of(xl, z, core, xh, y):
    return (((xl * 4 + z) * 2 + core) * 2 + xh) * 4 + y


def partners(orders, flips):
    pairs = []
    for xl in range(2):
        for z in range(4):
            for core in range(2):
                for xh in range(2):
                    for y in range(4):
                        place = {"x": xh * 2 + xl, "y": y, "z": z}
                        for axis, flip in zip(orders[core], flips):
                            place[axis] ^= flip
                        to = index_of(place["x"] % 2, place["z"], core, place["x"] // 2, place["y"])
                        pairs.append((index_of(xl, z, core, xh, y), to))
    return pairs


ORDERS = (("x", "y", "z"), ("y", "z", "x"))


def from_partners(held, flips):
    return lax.ppermute(held, ALL, partners(ORDERS, flips))


def from_line(held):
    return [from_partners(held, (0, 0, flip)) for flip in (1, 2, 3)]


def other_core(held):
    return lax.ppermute(held, "core", [(0, 1), (1, 0)])


def body(pair, chain_ids, block_mask, w_query, w_key, w_value, w_gate, w_bias, w_out):
    at = {name: lax.axis_index(name) for name in ALL}
    column = at["core"] * 64 + lax.axis_index(("xh", "y", "xl", "z"))
    mine = lax.dynamic_slice_in_dim(chain_ids.reshape(8, 128), column, 1, 1)
    lo = jnp.sum((chain_ids[None, :] < mine).astype(jnp.int32), axis=1)
    hi = jnp.sum((chain_ids[None, :] <= mine).astype(jnp.int32), axis=1)
    place = jnp.stack([at["xh"] * 2 + at["xl"], at["y"], at["z"], at["core"]] + [at["z"] * 0] * 4)
    info = jnp.stack([lo, hi, place]).astype(jnp.int32)
    normed, bias = norm_and_bias(pair, w_bias.T)
    held = jnp.concatenate([bias] + [from_partners(bias, (n, 0, 0)) for n in (1, 2, 3)], axis=0)
    held, info = lax.optimization_barrier((held, info))
    held = jnp.concatenate([held] + [from_partners(held, (0, n, 0)) for n in (1, 2, 3)], axis=0)
    held, normed = lax.optimization_barrier((held, normed))
    parts = [held] + from_line(held)
    parts = parts + [other_core(p) for p in parts]
    x = lax.all_to_all(normed, ("xh", "y", "xl", "z"), split_axis=0, concat_axis=0, tiled=True)
    weights = (w_query, w_key, w_value, w_gate, w_out)
    update = attend(info, block_mask, x.reshape(8, 8, 128, 128), weights, parts)
    back = lax.all_to_all(update, ("xh", "y", "xl", "z", "core"), split_axis=0, concat_axis=0, tiled=True)
    return put_in_order(back.reshape(128, 64, 128)).reshape(1, 1, 8, 1024, 128)


def solution(mesh):
    fine = Mesh(mesh.devices.reshape(SIZES), ALL)
    row, col = ("xl", "z", "core"), ("xh", "y")
    return jax.shard_map(
        body,
        mesh=fine,
        in_specs=(P(row, col, None), P(), P(), P(), P(), P(), P(), P(), P()),
        out_specs=P(col, row, None, None, None),
        check_vma=False,
    )
```

```python
import math

import jax
import jax.numpy as jnp
from jax import lax
from jax.experimental import pallas as pl
from jax.experimental.pallas import tpu as pltpu
from jax.sharding import Mesh, PartitionSpec as P

ALL = ("xl", "z", "core", "xh", "y")
SIZES = (2, 4, 2, 2, 4)
LOG2E = math.log2(math.e)
SCALE = 32.0 ** -0.5
LEAST = 1e-25
MOST = 1e30
STEP = 1024
NT = (((1,), (1,)), ((), ()))
F32 = jnp.float32
BF16 = jnp.bfloat16


def dot(a, b):
    return jnp.dot(a, b, preferred_element_type=F32)


def dot_nt(a, b):
    return lax.dot_general(a, b, NT, preferred_element_type=F32)


def layer_normed(narrow):
    ones = jnp.ones((384, 128), BF16)
    off = narrow.astype(F32) - dot(narrow, ones[:128]) * (1.0 / 128)
    left = off * off
    terms = []
    for _ in range(3):
        terms.append(left.astype(BF16))
        left = left - terms[-1].astype(F32)
    spread = dot(jnp.concatenate(terms, axis=1), ones) * (1.0 / 128)
    return (off * lax.rsqrt(spread + 1e-5)).astype(BF16)


def norm_kernel(pair_ref, wb_ref, normed_ref, bias_ref):
    rows = []
    for i in range(0, 32, 16):
        normed = layer_normed(pair_ref[i : i + 16].reshape(2048, 128))
        normed_ref[i : i + 16] = normed.reshape(16, 128, 128)
        biases = dot_nt(wb_ref[...], normed)
        rows += [biases[:, n * 128 : (n + 1) * 128] for n in range(16)]
    for h in range(4):
        bias_ref[0, h] = jnp.concatenate([r[h : h + 1] for r in rows], axis=0).astype(BF16)


def norm_and_bias(pair, wb):
    return pl.pallas_call(
        norm_kernel,
        grid=(2,),
        in_specs=[
            pl.BlockSpec((32, 128, 128), lambda g: (g, 0, 0)),
            pl.BlockSpec((4, 128), lambda g: (0, 0)),
        ],
        out_specs=[
            pl.BlockSpec((32, 128, 128), lambda g: (g, 0, 0)),
            pl.BlockSpec((1, 4, 32, 128), lambda g: (0, 0, g, 0)),
        ],
        out_shape=[
            jax.ShapeDtypeStruct((64, 128, 128), BF16),
            jax.ShapeDtypeStruct((1, 4, 64, 128), BF16),
        ],
    )(pair, wb)


def tile_in_use(info, mask, t, kt):
    return (mask[t, kt] == 1) | ((info[1, t] > kt * 128) & (info[0, t] < kt * 128 + 128))


def attend_kernel(info, mask, x_hbm, wq, wk, wv, wg, wo, a0, a1, a2, a3, a4, a5, a6, a7,
                  out_hbm, x_ref, out_ref, tiles, w_s, q_ref, k_ref, v_ref, gates, bias_s, kb0, kb1, vb0, vb1, p0, p1, acc, top, sems, x_sems, out_sems):
    copies = [
        pltpu.make_async_copy(ref, bias_s.at[pl.ds(n * 16, 16)], sems.at[n])
        for n, ref in enumerate((a0, a1, a2, a3, a4, a5, a6, a7))
    ]
    def rows_of(t):
        return pltpu.make_async_copy(x_hbm.at[:, t], x_ref.at[:, t], x_sems.at[t])

    for t in range(8):
        rows_of(t).start()
    for copy in copies:
        copy.start()
    px, py, pz, core = info[2, 0], info[2, 1], info[2, 2], info[2, 3]
    here = (core * 64 + pz * 16 + py * 4 + px, (1 - core) * 64 + px * 16 + pz * 4 + py)
    lane = lax.broadcasted_iota(jnp.int32, (128, 128), 1) // 32
    spot = lax.broadcasted_iota(jnp.int32, (128, 128), 0)
    spot_lanes = lax.broadcasted_iota(jnp.int32, (64, 128), 1)

    def add(e, n):
        tiles[n] = e
        return n + tile_in_use(info, mask, e // 8, e % 8).astype(jnp.int32)

    count = lax.fori_loop(0, 64, add, 0)
    tiles[count] = -1
    tiles[count + 1] = -1

    w_s[0] = jnp.concatenate([wk[...], wv[...]], axis=1)
    w_s[1] = jnp.concatenate([wq[...], wg[...]], axis=1)

    def project(t, carry):
        rows_of(t).wait()
        both = dot(x_ref[:, t].reshape(1024, 128), w_s[0]).astype(BF16)
        k_ref[t] = both[:, :128]
        v_ref[t] = both[:, 128:]
        both = dot(x_ref[:, t].reshape(1024, 128), w_s[1])
        q_ref[t] = both[:, :128].astype(BF16)
        gates[t] = 1.0 / (1.0 + jnp.exp2(both[:, 128:] * -LOG2E))
        acc[t] = jnp.zeros((1024, 256), F32)
        return carry

    lax.fori_loop(0, 8, project, 0)

    def bounds(t, kt, valid):
        whole = (mask[t, kt] == 1) & valid
        lo = jnp.where(valid, jnp.where(whole, 0, info[0, t]), 5000)
        hi = jnp.where(valid, jnp.where(whole, 5000, info[1, t]), 0)
        return lo - kt * 128, hi - kt * 128

    def entry(n):
        e = tiles[n]
        held = jnp.maximum(e, 0)
        return held // 8, held % 8, e >= 0

    def block(ref, t, kt):
        return ref[t, pl.ds(pl.multiple_of(kt * 128, 128), 128), :]

    def pack_keys(t, kt, kb):
        keys = block(k_ref, t, kt)
        for h in range(4):
            kb[h * 128 : (h + 1) * 128, :] = jnp.where(lane == h, keys, jnp.zeros_like(keys))

    def pack_values(t, kt, valid, vb):
        lo, hi = bounds(t, kt, valid)
        allowed = (spot >= lo) & (spot < hi)
        values = block(v_ref, t, kt).astype(F32)
        for h in range(4):
            mine = (lane == h) & allowed
            vb[h * 128 : (h + 1) * 128, :128] = jnp.where(mine, values, 0.0).astype(BF16)
            vb[h * 128 : (h + 1) * 128, 128:] = jnp.where(mine, 1.0, 0.0).astype(BF16)

    def bias_tiles(g, kt):
        xl, z = g // 4, g % 4
        xh, y = kt // 4, kt % 4
        at0 = here[0] ^ (z * 16 + xl) ^ (y * 4 + xh * 2)
        at1 = here[1] ^ (xl * 16 + z * 4) ^ (xh * 32 + y)
        return at0, at1

    def scores(s, at, h):
        return (s * SCALE + bias_s[at, h].astype(F32)) * LOG2E

    def scored(t, kt, kb, use, first, count):
        s = dot_nt(q_ref[t, first : first + count, :], kb[...])
        for g in range(count // 128):
            for part, at in enumerate(bias_tiles(first // 128 + g, kt)):
                start = g * 128 + part * 64
                for h in range(4):
                    z = scores(s[start : start + 64, h * 128 : (h + 1) * 128], at, h)
                    use(slice(first + start, first + start + 64), h, z)

    def weigh(t, kt, kb, p, first, count):
        def seen(rows, h, z):
            p[rows, h * 128 : (h + 1) * 128] = jnp.exp2(z).astype(BF16)

        scored(t, kt, kb, seen, first, count)

    def mix(t, vb, p, first, count):
        rows = slice(first, first + count)
        acc[t, rows, :] += dot(p[rows, :], vb[...])

    p1[...] = jnp.zeros_like(p1)
    vb1[...] = jnp.zeros_like(vb1)
    t, kt, _ = entry(0)
    pack_keys(t, kt, kb0)
    for copy in copies:
        copy.wait()

    def two(m, carry):
        t0, kt0, valid0 = entry(2 * m)
        t1, kt1, valid1 = entry(2 * m + 1)
        t2, kt2, _ = entry(jnp.minimum(2 * m + 2, count))
        before, _, _ = entry(jnp.maximum(2 * m - 1, 0))
        for first in range(0, 1024, STEP):
            mix(before, vb1, p1, first, STEP)
            weigh(t0, kt0, kb0, p0, first, STEP)
        pack_values(t0, kt0, valid0, vb0)
        pack_keys(t1, kt1, kb1)
        for first in range(0, 1024, STEP):
            mix(t0, vb0, p0, first, STEP)
            weigh(t1, kt1, kb1, p1, first, STEP)
        pack_values(t1, kt1, valid1, vb1)
        pack_keys(t2, kt2, kb0)
        return carry

    pairs = (count + 1) // 2
    lax.fori_loop(0, pairs, two, 0)
    last, _, _ = entry(2 * pairs - 1)
    mix(last, vb1, p1, 0, 1024)

    def redo(t):
        top[...] = jnp.full_like(top, -3e38)
        acc[t] = jnp.zeros((1024, 256), F32)

        def per_tile(body):
            def step(kt, carry):
                @pl.when(tile_in_use(info, mask, t, kt))
                def _():
                    pack_keys(t, kt, kb0)
                    pack_values(t, kt, True, vb0)
                    body(kt)

                return carry

            lax.fori_loop(0, 8, step, 0)

        def find_top(kt):
            lo, hi = bounds(t, kt, True)
            allowed = (spot_lanes >= lo) & (spot_lanes < hi)

            def seen(rows, h, z):
                top[h, rows, :] = jnp.maximum(top[h, rows, :], jnp.where(allowed, z, -3e38))

            for first in range(0, 1024, STEP):
                scored(t, kt, kb0, seen, first, STEP)

        def add_up(kt):
            def seen(rows, h, z):
                p = jnp.exp2(jnp.minimum(z - top[h, rows, :], 0.0))
                p0[rows, h * 128 : (h + 1) * 128] = p.astype(BF16)

            for first in range(0, 1024, STEP):
                scored(t, kt, kb0, seen, first, STEP)
            mix(t, vb0, p0, 0, 1024)

        per_tile(find_top)
        for h in range(4):
            top[h] = jnp.broadcast_to(jnp.max(top[h], axis=-1, keepdims=True), (1024, 128))
        per_tile(add_up)

    def worst(t):
        total = acc[t, :, 128:]
        bad = jnp.where((total > LEAST) & (total < MOST), 0.0, 1.0)
        return jnp.max(bad.reshape(128, 8, 128), axis=0)

    def check(t, carry):
        @pl.when(jnp.max(worst(t)) > 0.5)
        def _():
            redo(t)

        return carry

    any_bad = lax.fori_loop(0, 8, lambda t, m: jnp.maximum(m, worst(t)), jnp.zeros((8, 128), F32))

    @pl.when(jnp.max(any_bad) > 0.5)
    def _():
        lax.fori_loop(0, 8, check, 0)

    def part_out(pair):
        return pltpu.make_async_copy(out_ref.at[pair], out_hbm.at[:, pair], out_sems.at[pair])

    for pair in range(4):
        updates = []
        for t in (2 * pair, 2 * pair + 1):
            a = acc[t]
            gated = (gates[t] * (a[:, :128] / a[:, 128:])).astype(BF16)
            updates.append(dot(gated, wo[...]).reshape(128, 8, 128))
        out_ref[pair] = jnp.concatenate(updates, axis=1).astype(BF16)
        part_out(pair).start()
    for pair in range(4):
        part_out(pair).wait()


def attend(info, mask, x, weights, bias_parts):
    smem = pl.BlockSpec(memory_space=pltpu.SMEM)
    vmem = pl.BlockSpec(memory_space=pltpu.VMEM)
    hbm = pl.BlockSpec(memory_space=pl.ANY)
    return pl.pallas_call(
        attend_kernel,
        in_specs=[smem, smem, hbm] + [vmem] * 5 + [hbm] * 8,
        out_specs=hbm,
        out_shape=jax.ShapeDtypeStruct((128, 4, 16, 128), BF16),
        scratch_shapes=[
            pltpu.VMEM((8, 8, 128, 128), BF16),
            pltpu.VMEM((4, 128, 16, 128), BF16),
            pltpu.SMEM((72,), jnp.int32),
            pltpu.VMEM((2, 128, 256), BF16),
            pltpu.VMEM((8, 1024, 128), BF16),
            pltpu.VMEM((8, 1024, 128), BF16),
            pltpu.VMEM((8, 1024, 128), BF16),
            pltpu.VMEM((8, 1024, 128), F32),
            pltpu.VMEM((128, 4, 64, 128), BF16),
            pltpu.VMEM((512, 128), BF16),
            pltpu.VMEM((512, 128), BF16),
            pltpu.VMEM((512, 256), BF16),
            pltpu.VMEM((512, 256), BF16),
            pltpu.VMEM((1024, 512), BF16),
            pltpu.VMEM((1024, 512), BF16),
            pltpu.VMEM((8, 1024, 256), F32),
            pltpu.VMEM((4, 1024, 128), F32),
            pltpu.SemaphoreType.DMA((8,)),
            pltpu.SemaphoreType.DMA((8,)),
            pltpu.SemaphoreType.DMA((4,)),
        ],
        compiler_params=pltpu.CompilerParams(vmem_limit_bytes=63 * 2**20),
        cost_estimate=pl.CostEstimate(flops=20 * 10**9, bytes_accessed=12 * 2**20, transcendentals=11 * 10**6),
    )(info, mask, x, *weights, *bias_parts)


def order_kernel(in_ref, out_ref):
    for t in range(2):
        held = in_ref[:, t * 8 : t * 8 + 8, :].astype(F32).reshape(64, 2, 8, 128)
        for core in range(2):
            turned = jnp.swapaxes(held[:, core], 0, 1)
            out_ref[:, t * 128 + core * 64 : t * 128 + core * 64 + 64, :] = turned.astype(BF16)


def put_in_order(received):
    return pl.pallas_call(
        order_kernel,
        grid=(4,),
        in_specs=[pl.BlockSpec((128, 16, 128), lambda g: (0, g, 0))],
        out_specs=pl.BlockSpec((8, 256, 128), lambda g: (0, g, 0)),
        out_shape=jax.ShapeDtypeStruct((8, 1024, 128), BF16),
        compiler_params=pltpu.CompilerParams(vmem_limit_bytes=32 * 2**20),
    )(received)


def index_of(xl, z, core, xh, y):
    return (((xl * 4 + z) * 2 + core) * 2 + xh) * 4 + y


def partners(orders, flips):
    pairs = []
    for xl in range(2):
        for z in range(4):
            for core in range(2):
                for xh in range(2):
                    for y in range(4):
                        place = {"x": xh * 2 + xl, "y": y, "z": z}
                        for axis, flip in zip(orders[core], flips):
                            place[axis] ^= flip
                        to = index_of(place["x"] % 2, place["z"], core, place["x"] // 2, place["y"])
                        pairs.append((index_of(xl, z, core, xh, y), to))
    return pairs


ORDERS = (("x", "y", "z"), ("y", "z", "x"))


def from_partners(held, flips):
    return lax.ppermute(held, ALL, partners(ORDERS, flips))


def from_line(held):
    return [from_partners(held, (0, 0, flip)) for flip in (1, 2, 3)]


def other_core(held):
    return lax.ppermute(held, "core", [(0, 1), (1, 0)])


def body(pair, chain_ids, block_mask, w_query, w_key, w_value, w_gate, w_bias, w_out):
    at = {name: lax.axis_index(name) for name in ALL}
    column = at["core"] * 64 + lax.axis_index(("xh", "y", "xl", "z"))
    mine = lax.dynamic_slice_in_dim(chain_ids.reshape(8, 128), column, 1, 1)
    lo = jnp.sum((chain_ids[None, :] < mine).astype(jnp.int32), axis=1)
    hi = jnp.sum((chain_ids[None, :] <= mine).astype(jnp.int32), axis=1)
    place = jnp.stack([at["xh"] * 2 + at["xl"], at["y"], at["z"], at["core"]] + [at["z"] * 0] * 4)
    info = jnp.stack([lo, hi, place]).astype(jnp.int32)
    normed, bias = norm_and_bias(pair, w_bias.T)
    held = jnp.concatenate([bias] + [from_partners(bias, (n, 0, 0)) for n in (1, 2, 3)], axis=0)
    held, info = lax.optimization_barrier((held, info))
    held = jnp.concatenate([held] + [from_partners(held, (0, n, 0)) for n in (1, 2, 3)], axis=0)
    held, normed = lax.optimization_barrier((held, normed))
    parts = [held] + from_line(held)
    parts = parts + [other_core(p) for p in parts]
    x = lax.all_to_all(normed, ("xh", "y", "xl", "z"), split_axis=0, concat_axis=0, tiled=True)
    weights = (w_query, w_key, w_value, w_gate, w_out)
    update = attend(info, block_mask, x.reshape(8, 8, 128, 128), weights, parts)
    back = lax.all_to_all(update, ("xh", "y", "xl", "z", "core"), split_axis=0, concat_axis=0, tiled=True)
    return put_in_order(back.reshape(128, 64, 128)).reshape(1, 1, 8, 1024, 128)


def solution(mesh):
    fine = Mesh(mesh.devices.reshape(SIZES), ALL)
    row, col = ("xl", "z", "core"), ("xh", "y")
    return jax.shard_map(
        body,
        mesh=fine,
        in_specs=(P(row, col, None), P(), P(), P(), P(), P(), P(), P(), P()),
        out_specs=P(col, row, None, None, None),
        check_vma=False,
    )
```
